32 devices in a mesh: narrow: 4 (over z), wide: 8 (over y, x, core).
Axes of the slice: x: 2, y: 2, z: 4, core: 2. Of those that a mesh axis runs over, the one named last changes fastest.
Arguments:
- layer_in: bfloat16 [16384, 1024], P(('narrow', 'wide')), may hold values from -30 to 30
- first_values: bfloat16 [16384, 1024], P(('narrow', 'wide')), may hold values from -6 to 6
- out_grad: bfloat16 [16384, 1024], P(('narrow', 'wide')), may hold values from -6 to 6
- seq_group: int32 [32], P(('narrow', 'wide')), may hold values from 0 to 1
- short_split: int32 [32], P(('narrow', 'wide')), may hold values from 128 to 384
- attn_gain: bfloat16 [1024], P(('narrow', 'wide')), may hold values from 0.099609375 to 1.8984375
- mlp_gain: bfloat16 [1024], P(('narrow', 'wide')), may hold values from 0.099609375 to 1.8984375
- w_query: bfloat16 [1024, 1024], P(('narrow', 'wide')), may hold values from -0.1875 to 0.1875
- w_key: bfloat16 [1024, 1024], P(('narrow', 'wide')), may hold values from -0.1875 to 0.1875
- w_value: bfloat16 [1024, 1024], P(('narrow', 'wide')), may hold values from -0.1875 to 0.1875
- w_out: bfloat16 [1024, 1024], P(None, ('narrow', 'wide')), may hold values from -2 to 2
- w_gate: bfloat16 [1024, 2816], P('wide', 'narrow'), may hold values from -0.1875 to 0.1875
- w_up: bfloat16 [1024, 2816], P('wide', 'narrow'), may hold values from -0.1875 to 0.1875
- w_down: bfloat16 [2816, 1024], P('narrow', 'wide'), may hold values from -0.109375 to 0.109375
Outputs:
- layer_out: bfloat16 [16384, 1024], P(('narrow', 'wide'))
- in_grad: float32 [16384, 1024], P(('narrow', 'wide'))
- first_values_grad: float32 [16384, 1024], P(('narrow', 'wide'))
- attn_gain_grad: float32 [1024], P(('narrow', 'wide'))
- mlp_gain_grad: float32 [1024], P(('narrow', 'wide'))
- w_query_grad: float32 [1024, 1024], P(('narrow', 'wide'))
- w_key_grad: float32 [1024, 1024], P(('narrow', 'wide'))
- w_value_grad: float32 [1024, 1024], P(('narrow', 'wide'))
- w_out_grad: float32 [1024, 1024], P(None, ('narrow', 'wide'))
- w_gate_grad: float32 [1024, 2816], P('wide', 'narrow')
- w_up_grad: float32 [1024, 2816], P('wide', 'narrow')
- w_down_grad: float32 [2816, 1024], P('narrow', 'wide')
The draws below stay inside these ranges and needn't reach their ends.
Inputs may be any that keep to these rules, and one draw needn't show every extreme that they name: `short_split`: used only in slots whose seq_group is 1.
All inputs are finite; a program needn't handle non-finite values.
Results may differ from the reference program's by a relative error of at most 0.014.
Values may be sent and summed in bfloat16 or wider, within the bound.
No kernel may reach another device: no remote copies, remote signals or barrier semaphores. Data moves between devices by JAX's collectives and lax.ppermute only.
A program may use at most 192 MiB of HBM per device.

```python
import math
from functools import partial
import jax
import jax.numpy as jnp
from jax import lax

D = 1024
HEADS = 16
FF = 2816
TOK_DEV = 512
TOKENS = 16384
SLOTS = 32


def draw_layer_in(key, part):
    key = jax.random.fold_in(key, 11)
    key_base, key_rows, key_cols = jax.random.split(key, 3)
    base = jnp.clip(jax.random.normal(key_base, (TOKENS, D), jnp.float32), -4.0, 4.0)
    row_scale = jnp.exp(jax.random.uniform(key_rows, (TOKENS, 1), jnp.float32, math.log(0.3), math.log(3.0)))
    col_scale = jnp.exp(jax.random.uniform(key_cols, (1, D), jnp.float32, math.log(0.4), math.log(2.5)))
    return (base * row_scale * col_scale).astype(jnp.bfloat16)


def place_ends(entries, rng, smallest, high):
    longest = entries.shape.index(max(entries.shape))
    spots = []
    for shift in (0, 1):
        where = [jax.random.randint(jax.random.fold_in(rng, axis), (), 0, length) for axis, length in enumerate(entries.shape)]
        where[longest] = (where[longest] + shift) % entries.shape[longest]
        spots.append(tuple(where))
    return entries.at[spots[0]].set(smallest).at[spots[1]].set(high)


def spiked(array, own_key, source, target, shards_of, factor):
    owner, partner = [(jnp.arange(array.shape[dim]) // (array.shape[dim] // shards_of)).reshape([-1 if axis == dim else 1 for axis in range(array.ndim)]) for dim in (source, target)]
    chosen = jax.random.permutation(own_key, shards_of)[partner]
    strong = (owner == chosen) | (owner == (partner + shards_of // 2) % shards_of)
    return jnp.where(strong, factor * array, array)


def level_of(own_key, extent, shards, least, top_value):
    def one(position, shards_of):
        heights = jax.random.uniform(jax.random.fold_in(jax.random.fold_in(own_key, 6), position), (shards_of,), jnp.float32, least / len(shards), top_value / len(shards))
        return jnp.repeat(jnp.exp(heights), extent[position] // shards_of).reshape((-1,) + (1,) * (len(extent) - position - 1))

    loudness = one(*shards[0])
    for cut in shards[1:]:
        loudness = loudness * one(*cut)
    return loudness


def centred(own_key, extent, width, most, cuts=(), kind=jnp.bfloat16):
    loudness = level_of(own_key, extent, cuts, -0.22, 0.18) if cuts else 1.0
    values = jax.random.normal(own_key, extent, jnp.float32) * width * loudness
    return jnp.minimum(jnp.maximum(values, -most), most).astype(kind)


def gaussian_with(key, dims, deviation, bound, shards, heavy, kind=jnp.bfloat16):
    drawn = deviation * jax.random.normal(key, dims, jnp.float32)
    if shards:
        drawn = drawn * level_of(key, dims, shards, -0.22, 0.18)
    return jnp.clip(spiked(drawn, jax.random.fold_in(key, 3), *heavy), -bound, bound).astype(kind)


def setup_inputs(seed: int = 0) -> dict:
    seeds = jax.random.split(jax.random.key(seed), 15)
    return {
        "layer_in": draw_layer_in(jax.random.fold_in(seeds[14], 71), 0),
        "first_values": centred(seeds[1], (TOKENS, D), 1.0, 6.0, ((0, 32),)),
        "out_grad": gaussian_with(seeds[2], (TOKENS, D), 1.0, 6.0, ((0, 32),), (0, 1, 32, 2.75)),
        "seq_group": place_ends(jax.random.randint(seeds[3], (SLOTS,), 0, 2), jax.random.fold_in(seeds[3], 1), 0, 1).astype(jnp.int32),
        "short_split": place_ends(jax.random.randint(seeds[4], (SLOTS,), TOK_DEV // 4, 3 * TOK_DEV // 4 + 1), jax.random.fold_in(seeds[4], 1), TOK_DEV // 4, (3 * TOK_DEV // 4 + 1) - 1).astype(jnp.int32),
        "attn_gain": jnp.clip(1.0 + 0.18 * jax.random.normal(seeds[5], (D,), jnp.float32), 0.099609375, 1.8984375).astype(jnp.bfloat16),
        "mlp_gain": jnp.clip(1.0 + 0.18 * jax.random.normal(seeds[6], (D,), jnp.float32), 0.099609375, 1.8984375).astype(jnp.bfloat16),
        "w_query": centred(seeds[7], (D, D), D ** -0.5, 0.1875, ((0, 32),)),
        "w_key": centred(seeds[8], (D, D), D ** -0.5, 0.1875, ((0, 32),)),
        "w_value": centred(seeds[9], (D, D), D ** -0.5, 0.1875, ((0, 32),)),
        "w_out": centred(seeds[10], (D, D), (D // 128) ** -0.5, 2.0, ((1, 32),)),
        "w_gate": centred(seeds[11], (D, FF), D ** -0.5, 0.1875, ((0, 8), (1, 4))),
        "w_up": centred(seeds[12], (D, FF), D ** -0.5, 0.1875, ((0, 8), (1, 4))),
        "w_down": centred(seeds[13], (FF, D), FF ** -0.5, 0.109375, ((0, 4), (1, 8))),
    }


epsilon = 1e-06
highest = lax.Precision.HIGHEST

@jax.custom_vjp
def low(v):
    return lax.optimization_barrier(v.astype(jnp.bfloat16)).astype(jnp.float32)

@jax.custom_vjp
def low_back(v):
    return v

def low_keep(v):
    return (low(v), None)

def low_pass(kept, grad):
    return (grad,)

def back_keep(v):
    return (v, None)

def back_low(kept, grad):
    return (low(grad),)
low.defvjp(low_keep, low_pass)
low_back.defvjp(back_keep, back_low)

def rms_scale(values):
    return lax.rsqrt(lax.optimization_barrier(jnp.mean(values * values, axis=-1, keepdims=True)) + epsilon)

def angles(positions, head_dim):
    half_dim = head_dim // 2
    frequency = jnp.exp(jnp.arange(half_dim, dtype=jnp.float32) * (-2.0 * math.log(10000.0) / head_dim))
    turned = positions[:, None] * frequency[None, :]
    return (jnp.cos(turned)[:, None, :], jnp.sin(turned)[:, None, :])

def rotate(values, cos_table, sin_table):
    half_dim = values.shape[-1] // 2
    first_half = values[..., :half_dim]
    second_half = values[..., half_dim:]
    return jnp.concatenate([first_half * cos_table - second_half * sin_table, second_half * cos_table + first_half * sin_table], axis=-1)

def project(left, right):
    return jnp.dot(left, right, precision=highest, preferred_element_type=jnp.float32)

def layer_group(params, rows_in, values_in, split_rows):
    gain_attn, gain_mlp, w_query, w_key, w_value, w_out, w_gate, w_up, w_down = params
    slot_count = split_rows.shape[0]
    total_rows, model_width = rows_in.shape
    slot_rows = total_rows // slot_count
    head_count = HEADS
    head_dim = model_width // head_count
    row_index = jnp.arange(slot_rows, dtype=jnp.int32)
    second = row_index[None, :] >= split_rows[:, None]
    positions = jnp.where(second, row_index[None, :] - split_rows[:, None], row_index[None, :])
    positions = positions.astype(jnp.float32).reshape(total_rows)
    cos_table, sin_table = angles(positions, head_dim)
    normed = low(rows_in * rms_scale(rows_in) * gain_attn)
    queries = low_back(project(normed, w_query)).reshape(total_rows, head_count, head_dim)
    key_rows = low_back(project(normed, w_key)).reshape(total_rows, head_count, head_dim)
    queries = low(rotate(queries, cos_table, sin_table)).reshape(slot_count, slot_rows, head_count, head_dim)
    key_rows = low(rotate(key_rows, cos_table, sin_table)).reshape(slot_count, slot_rows, head_count, head_dim)
    mixed_values = low(0.5 * low_back(project(normed, w_value)) + 0.5 * values_in)
    mixed_values = mixed_values.reshape(slot_count, slot_rows, head_count, head_dim)
    scores = low_back(jnp.einsum('sqhd,skhd->shqk', queries, key_rows, precision=highest)) * head_dim ** (-0.5)
    causal = row_index[:, None] >= row_index[None, :]
    allowed = (second[:, :, None] == second[:, None, :]) & causal[None]
    scores = jnp.where(allowed[:, None], scores, -1e+30)
    row_max = lax.optimization_barrier(jnp.max(scores, axis=-1, keepdims=True))
    exponent = jnp.exp(scores - row_max)
    weights = low(exponent / lax.optimization_barrier(jnp.sum(exponent, axis=-1, keepdims=True)))
    attended = jnp.einsum('shqk,skhd->sqhd', weights, mixed_values, precision=highest).reshape(total_rows, model_width)
    attended = low_back(low(attended))
    hidden_in = rows_in + low_back(project(attended, w_out))
    normed_two = low(hidden_in * rms_scale(hidden_in) * gain_mlp)
    gate_proj = low_back(project(normed_two, w_gate))
    up_proj = low_back(project(normed_two, w_up))
    active = low(jax.nn.silu(gate_proj) * up_proj)
    return hidden_in + low_back(project(active, w_down))

def reference(layer_in, first_values, out_grad, seq_group, short_split, attn_gain, mlp_gain, w_query, w_key, w_value, w_out, w_gate, w_up, w_down):
    slot_count = layer_in.shape[0] // TOK_DEV
    per_group = math.gcd(slot_count, max(1, 2048 // TOK_DEV))
    group_count = slot_count // per_group
    group_rows = per_group * TOK_DEV
    split_rows = jnp.where(seq_group == 0, TOK_DEV, short_split).astype(jnp.int32)
    params = tuple((weight.astype(jnp.float32) for weight in (attn_gain, mlp_gain, w_query, w_key, w_value, w_out, w_gate, w_up, w_down)))
    rows_float = layer_in.astype(jnp.float32)
    values_float = first_values.astype(jnp.float32)

    def whole_layer(weights_in, rows_in, values_in):
        checked = jax.checkpoint(partial(layer_group, weights_in))

        def apply_group(group_input):
            return checked(group_input[0], group_input[1], group_input[2])
        results = lax.map(apply_group, (rows_in.reshape(group_count, group_rows, -1), values_in.reshape(group_count, group_rows, -1), split_rows.reshape(group_count, per_group)))
        return results.reshape(rows_in.shape)
    result, pullback = jax.vjp(whole_layer, params, rows_float, values_float)
    param_grads, rows_grad, values_grad = pullback(out_grad.astype(jnp.float32))
    return (result.astype(jnp.bfloat16), rows_grad, values_grad, param_grads[0], param_grads[1], param_grads[2], param_grads[3], param_grads[4], param_grads[5], param_grads[6], param_grads[7], param_grads[8])
```

```python
import math

import jax
import jax.numpy as jnp
from jax import lax
from jax.experimental import pallas as pl
from jax.experimental.pallas import tpu as pltpu
from jax.sharding import PartitionSpec as P

HEAD_DIM = 64
EPS = 1e-06
BF = jnp.bfloat16
F32 = jnp.float32
NARROW, WIDE = "narrow", "wide"
VMEM = 60


def dot(left, right, dims):
    return lax.dot_general(left, right, (dims, ((), ())), preferred_element_type=F32)


def nn(left, right):
    return dot(left, right, ((1,), (0,)))


def nt(left, right):
    return dot(left, right, ((1,), (1,)))


def tn(left, right):
    return dot(left, right, ((0,), (0,)))


def rms_scale(values):
    return lax.rsqrt(jnp.mean(values * values, axis=-1, keepdims=True) + EPS)


def tile_of(rows):
    return min(256, rows)


def anywhere():
    return pl.BlockSpec(memory_space=pl.ANY)


def in_smem():
    return pl.BlockSpec(memory_space=pltpu.SMEM)


def in_vmem():
    return pl.BlockSpec(memory_space=pltpu.VMEM)


def params(mib):
    return pltpu.CompilerParams(vmem_limit_bytes=mib * 1024 * 1024)


def cost(flops, moved):
    return pl.CostEstimate(
        flops=int(2 * flops), bytes_accessed=int(moved), transcendentals=0
    )


def turn(v, cos, sin):
    lane = lax.broadcasted_iota(jnp.int32, v.shape, 1)
    swapped = jnp.where(
        lane % HEAD_DIM < HEAD_DIM // 2,
        pltpu.roll(v, 128 - HEAD_DIM // 2, 1),
        pltpu.roll(v, HEAD_DIM // 2, 1),
    )
    return v * cos + swapped * sin


def assemble(core, mine, came, shard):
    half = mine.shape[1]

    def body(core_ref, mine_ref, came_ref, out_ref):
        own, other = mine_ref[...].astype(F32), came_ref[...].astype(F32)
        first = core_ref[0] == 0
        lower, upper = jnp.where(first, own, other), jnp.where(first, other, own)
        for k in range(4):
            at = slice(k * shard, (k + 1) * shard)
            pair = jnp.concatenate([lower[at], upper[at]], 0)
            out_ref[2 * k * shard : 2 * (k + 1) * shard] = pair.astype(BF)
        row = lax.broadcasted_iota(jnp.int32, (16, half), 0)
        spare = jnp.where(row == 0, lower[4 * shard : 4 * shard + 1], upper[4 * shard : 4 * shard + 1])
        out_ref[8 * shard :] = spare.astype(BF)

    return pl.pallas_call(
        body,
        out_shape=jax.ShapeDtypeStruct((8 * shard + 16, half), BF),
        in_specs=[in_smem(), in_vmem(), in_vmem()],
        out_specs=in_vmem(),
        compiler_params=params(VMEM),
    )(core, mine, came)


def project_rows(xhat, fv2, cos, sin, near, far, spots, block, deps=()):
    count, depth = len(near), far[0].shape[0] + 1
    blocks = count * depth
    rows, width = xhat.shape
    half = fv2.shape[1]
    tile = tile_of(rows)

    def body(spot_ref, x_ref, fv_ref, cos_ref, sin_ref, *refs):
        q_ref, k_ref, v_ref, w_ref, wo_ref, g_ref, sem = refs[2 * count + len(deps) :]
        copies = [[] for _ in range(5)]
        for k in range(5):
            for m in range(count):
                for d in range(depth):
                    i = m * depth + d
                    source = refs[m] if d == 0 else refs[count + m].at[d - 1]
                    size = block if k < 4 else 16
                    to = pl.ds(pl.multiple_of(spot_ref[i] * size, size), size)
                    out = w_ref.at[k, to] if k < 3 else (wo_ref if k == 3 else g_ref).at[to]
                    copies[k].append(
                        pltpu.make_async_copy(source.at[pl.ds(k * block, size)], out, sem.at[k, i])
                    )
                    copies[k][-1].start()

        for k, out in ((0, q_ref), (1, k_ref), (2, v_ref)):
            for c in copies[k]:
                c.wait()

            @pl.loop(0, rows // tile)
            def _(t):
                at = pl.ds(pl.multiple_of(t * tile, tile), tile)
                y = nn(x_ref[at], w_ref[k])
                if k == 2:
                    out[at] = (0.5 * y + 0.5 * fv_ref[at].astype(F32)).astype(BF)
                else:
                    factor = HEAD_DIM ** (-0.5) if k == 0 else 1.0
                    cos_t, sin_t = cos_ref[at] * factor, sin_ref[at] * factor
                    for g in range(half // 128):
                        lanes = slice(g * 128, g * 128 + 128)
                        out[at, lanes] = turn(y[:, lanes], cos_t, sin_t).astype(BF)

        for k in (3, 4):
            for c in copies[k]:
                c.wait()

    shape = jax.ShapeDtypeStruct((rows, half), BF)
    return pl.pallas_call(
        body,
        out_shape=(
            shape,
            shape,
            shape,
            jax.ShapeDtypeStruct((3, width, half), BF),
            jax.ShapeDtypeStruct((width, half), BF),
            jax.ShapeDtypeStruct((16 * blocks, half), BF),
        ),
        in_specs=[in_smem()] + [in_vmem()] * 4 + [anywhere()] * (2 * count + len(deps)),
        out_specs=[in_vmem()] * 6,
        scratch_shapes=[pltpu.SemaphoreType.DMA((5, blocks))],
        compiler_params=params(VMEM),
        cost_estimate=cost(6 * rows * width * half, 12e6),
    )(spots, xhat, fv2, cos, sin, *near, *far, *deps)


def query_blocks(rows):
    step = tile_of(rows)
    return [(s, step, s + step) for s in range(0, rows, step)]


def attend(splits, queries, keys, values, deps=()):
    rows2, half = queries.shape
    rows = rows2 // 2
    pairs = half // 128

    def body(split_ref, q_ref, k_ref, v_ref, *refs):
        o_ref, p_ref, bias = refs[len(deps) :]
        slot = pl.program_id(0)

        @pl.when(pl.program_id(1) == 0)
        def _():
            split = split_ref[slot]
            key = lax.broadcasted_iota(jnp.int32, (rows, rows), 0)
            query = lax.broadcasted_iota(jnp.int32, (rows, rows), 1)
            low = jnp.where(query >= split, split, 0)
            bias[...] = jnp.where((key <= query) & (key >= low), 0.0, -1e30)

        lane = lax.broadcasted_iota(jnp.int32, (rows, 128), 1)
        k_all = k_ref[...]
        v_t = v_ref[...].T
        feature = lax.broadcasted_iota(jnp.int32, (128, 1), 0)
        for start, count, key_end in query_blocks(rows):
            at = slice(start, start + count)
            q = q_ref[at]
            outs = []
            for h in range(2):
                in_head = (lane[:key_end] < 64) if h == 0 else (lane[:key_end] >= 64)
                k = jnp.where(in_head, k_all[:key_end], 0)
                s = nt(k, q) + bias[:key_end, at]
                e = jnp.exp(s - jnp.max(s, axis=0, keepdims=True))
                p = (e * (1.0 / jnp.sum(e, axis=0, keepdims=True))).astype(BF)
                p_ref[h, :key_end, at] = p
                outs.append(nn(v_t[:, :key_end], p))
            o_ref[at] = jnp.where(feature < 64, outs[0], outs[1]).astype(BF).T

    spec = pl.BlockSpec((rows, 128), lambda s, p, *_: (s, p))
    return pl.pallas_call(
        body,
        out_shape=(
            jax.ShapeDtypeStruct((rows2, half), BF),
            jax.ShapeDtypeStruct((4 * pairs, rows, rows), BF),
        ),
        grid_spec=pltpu.PrefetchScalarGridSpec(
            num_scalar_prefetch=1,
            grid=(2, pairs),
            in_specs=[spec] * 3 + [anywhere()] * len(deps),
            out_specs=[
                spec,
                pl.BlockSpec((2, rows, rows), lambda s, p, *_: (s * pairs + p, 0, 0)),
            ],
            scratch_shapes=[pltpu.VMEM((rows, rows), F32)],
        ),
        compiler_params=params(VMEM),
        cost_estimate=cost(16 * rows * rows * half, 12e6),
    )(splits, queries, keys, values, *deps)


def attend_back(queries, keys, values, weights, grad_att, cos, sin, start, pairs, deps=()):
    rows2, half = queries.shape
    rows = rows2 // 2
    all_pairs = half // 128

    def body(q_ref, k_ref, v_ref, p_ref, ga_ref, cos_ref, sin_ref, *refs):
        gq_ref, gk_ref, gv_ref, gk_sc, gv_sc = refs[len(deps) :]
        lane = lax.broadcasted_iota(jnp.int32, (rows, 128), 1)
        v_all = v_ref[...]
        k_t = k_ref[...].T
        feature = lax.broadcasted_iota(jnp.int32, (128, 1), 0)
        cos_all, sin_all = cos_ref[...], sin_ref[...]
        gk_sc[...] = jnp.zeros_like(gk_sc)
        gv_sc[...] = jnp.zeros_like(gv_sc)
        for start, count, key_end in query_blocks(rows):
            at = slice(start, start + count)
            ga, q = ga_ref[at], q_ref[at]
            outs = []
            for h in range(2):
                in_head = (lane[:key_end] < 64) if h == 0 else (lane[:key_end] >= 64)
                v = jnp.where(in_head, v_all[:key_end], 0)
                p = p_ref[h, :key_end, at]
                pf = p.astype(F32)
                gp = nt(v, ga)
                delta = jnp.sum(gp * pf, axis=0, keepdims=True)
                gs = (pf * (gp - delta)).astype(BF)
                gk_sc[h, :key_end] += nn(gs, q)
                gv_sc[h, :key_end] += nn(p, ga)
                outs.append(nn(k_t[:, :key_end], gs))
            gq = (jnp.where(feature < 64, outs[0], outs[1]) * HEAD_DIM ** (-0.5)).T
            gq_ref[at] = turn(gq, cos_all[at], -sin_all[at]).astype(BF)
        gk = jnp.where(lane < 64, gk_sc[0], gk_sc[1])
        gk_ref[...] = turn(gk, cos_all, -sin_all).astype(BF)
        gv_ref[...] = 0.5 * jnp.where(lane < 64, gv_sc[0], gv_sc[1])

    spec = pl.BlockSpec((rows, 128), lambda s, p: (s, p + start))
    out = pl.BlockSpec((rows, 128), lambda s, p: (s, p))
    table = pl.BlockSpec((rows, 128), lambda s, p: (s, 0))
    return pl.pallas_call(
        body,
        out_shape=(
            jax.ShapeDtypeStruct((rows2, 128 * pairs), BF),
            jax.ShapeDtypeStruct((rows2, 128 * pairs), BF),
            jax.ShapeDtypeStruct((rows2, 128 * pairs), F32),
        ),
        grid=(2, pairs),
        in_specs=[spec] * 3
        + [pl.BlockSpec((2, rows, rows), lambda s, p: (s * all_pairs + p + start, 0, 0)), spec, table, table]
        + [anywhere()] * len(deps),
        out_specs=[out] * 3,
        scratch_shapes=[pltpu.VMEM((2, rows, 128), F32)] * 2,
        compiler_params=params(VMEM),
        cost_estimate=cost(32 * rows * rows * 128 * pairs, 8e6),
    )(queries, keys, values, weights, grad_att, cos, sin, *deps)


def feed_forward(chips, normed_two, og_own, og_other, parts, before=None, deps=()):
    count = len(parts)
    _, units, lanes = parts[0].shape
    rows, width = normed_two.shape
    tile = min(512, rows // 2)
    tiles = rows // tile
    more = 0 if before is None else 3
    groups = min(2, count)
    low = count // groups

    def body(chip_ref, nt_hbm, og_first, og_second, *refs):
        ins = refs[:count]
        olds = refs[count : count + more]
        refs = refs[count + more + len(deps) :]
        br_outs, gn_hbm, outs = refs[:2], refs[2], refs[3 : 3 + groups]
        x_all, o_all, w, act, gg, gu, ob, br, gn, rsem, wsem, osem, psem = refs[3 + groups :]

        def lanes_at(m):
            if count == 1:
                return slice(None)
            return pl.ds(pl.multiple_of(chip_ref[m] * lanes, lanes), lanes)

        def rows_at(t):
            return pl.ds(t * tile, tile)

        row_in, weight_in, old_in = [], [], []
        per_core = tiles // 2

        def part_of(pair, t):
            return pair[t // per_core].at[rows_at(t % per_core)]

        for t in range(tiles):
            row_in.append((
                pltpu.make_async_copy(nt_hbm.at[rows_at(t)], x_all.at[rows_at(t)], rsem.at[0, t]),
                pltpu.make_async_copy(
                    part_of((og_first, og_second), t), o_all.at[rows_at(t)], rsem.at[1, t]
                ),
            ))
            old_in.append([])
            if more:
                old_in[t].append(
                    pltpu.make_async_copy(part_of(olds[:2], t), br.at[rows_at(t)], psem.at[0, t])
                )
                old_in[t].append(
                    pltpu.make_async_copy(olds[2].at[rows_at(t)], gn.at[rows_at(t)], psem.at[1, t])
                )
        for k in range(3):
            weight_in.append([
                pltpu.make_async_copy(ins[m].at[k], w.at[k, :, lanes_at(m)], wsem.at[k, m])
                for m in range(count)
            ])
        row_in[0][0].start()
        for k in range(3):
            for c in weight_in[k]:
                c.start()
            if k == 1:
                row_in[0][1].start()
        for t in range(1, tiles):
            row_in[t][0].start()
            row_in[t][1].start()
        for t in range(tiles):
            for c in old_in[t]:
                c.start()

        sends = []
        for t in range(tiles):
            at = rows_at(t)
            row_in[t][0].wait()
            x = x_all[at]
            if t == 0:
                for c in weight_in[0]:
                    c.wait()
            gate = nt(w[0], x)
            if t == 0:
                for c in weight_in[1]:
                    c.wait()
            up = nt(w[1], x)
            row_in[t][1].wait()
            if t == 0:
                for c in weight_in[2]:
                    c.wait()
            ga = nt(w[2], o_all[at])
            sig = jax.nn.sigmoid(gate)
            soft = gate * sig
            a = (soft * up).astype(BF)
            g = (ga * up * (sig + soft * (1.0 - sig))).astype(BF)
            u = (ga * soft).astype(BF)
            act[:, at] = a
            gg[:, at] = g
            gu[:, at] = u
            b = tn(a, w[2])
            n = tn(g, w[0]) + tn(u, w[1])
            if more:
                for c in old_in[t]:
                    c.wait()
                b = b + br[at].astype(F32)
                n = n + gn[at].astype(F32)
            br[at] = b.astype(BF)
            gn[at] = n.astype(BF)
            sends.append(pltpu.make_async_copy(br.at[at], part_of(br_outs, t), rsem.at[0, t]))
            sends.append(pltpu.make_async_copy(gn.at[at], gn_hbm.at[at], rsem.at[1, t]))
            sends[-2].start()
            sends[-1].start()

        for m in reversed(range(count)):
            at = lanes_at(m)
            x, o = x_all[:, at], o_all[:, at]
            for k, left, right in ((0, gg, x), (1, gu, x), (2, act, o)):
                ob[m, k] = nn(left[...], right).astype(BF)
            sends.append(pltpu.make_async_copy(ob.at[m], outs[m // low].at[m % low], osem.at[m]))
            sends[-1].start()
        for c in sends:
            c.wait()

    shape = jax.ShapeDtypeStruct((rows, width), BF)
    part_rows = jax.ShapeDtypeStruct((rows // 2, width), BF)
    part = jax.ShapeDtypeStruct((low,) + parts[0].shape, BF)
    out = pl.pallas_call(
        body,
        out_shape=(part_rows, part_rows, shape) + (part,) * groups,
        in_specs=[in_smem()] + [anywhere()] * (3 + count + more + len(deps)),
        out_specs=[anywhere()] * (3 + groups),
        scratch_shapes=[
            pltpu.VMEM((rows, width), BF),
            pltpu.VMEM((rows, width), BF),
            pltpu.VMEM((3, units, width), BF),
            pltpu.VMEM((units, rows), BF),
            pltpu.VMEM((units, rows), BF),
            pltpu.VMEM((units, rows), BF),
            pltpu.VMEM((count, 3, units, lanes), BF),
            pltpu.VMEM((rows, width), BF),
            pltpu.VMEM((rows, width), BF),
            pltpu.SemaphoreType.DMA((2, tiles)),
            pltpu.SemaphoreType.DMA((3, count)),
            pltpu.SemaphoreType.DMA((count,)),
            pltpu.SemaphoreType.DMA((2, tiles)),
        ],
        compiler_params=params(VMEM),
        cost_estimate=cost(18 * rows * width * units, 12e6),
    )(chips, normed_two, og_own, og_other, *parts, *(before or ()), *deps)
    return out[:3], list(out[3:])


def out_and_norm(x2, attended, att_other, out_mine, out_other, gain, deps=()):
    rows, width = x2.shape
    half = attended.shape[1]
    tile = tile_of(rows // 2)
    tiles = rows // tile

    def body(x_ref, a_ref, b_ref, wa_ref, wb_ref, gain_ref, *refs):
        h_ref, n_ref = refs[len(deps) :]
        h = x_ref[...].astype(F32) + nt(a_ref[...], wa_ref[...]) + nt(b_ref[...], wb_ref[...])
        h_ref[...] = h
        n_ref[...] = (h * rms_scale(h) * gain_ref[...]).astype(BF)

    def rows_of(width, shift=0):
        return pl.BlockSpec((tile, width), lambda t: ((t + shift) % tiles, 0))

    def whole(a):
        return pl.BlockSpec(a.shape, lambda t: (0, 0))

    return pl.pallas_call(
        body,
        out_shape=(
            jax.ShapeDtypeStruct((rows, width), F32),
            jax.ShapeDtypeStruct((rows, width), BF),
        ),
        grid=(tiles,),
        in_specs=[
            rows_of(width),
            rows_of(half),
            rows_of(half, tiles // 2),
            whole(out_mine),
            whole(out_other),
            whole(gain),
        ]
        + [anywhere()] * len(deps),
        out_specs=[rows_of(width)] * 2,
        compiler_params=params(VMEM),
        cost_estimate=cost(4 * rows * width * half, 12e6),
    )(x2, attended, att_other, out_mine, out_other, gain, *deps)


def norm_two_back(spots, grad_nt, grad_nt_other, hidden, og_own, og_other, gain, attended, out_mine, block, labels, deps=()):
    rows, width = hidden.shape
    half = attended.shape[1]
    tile = tile_of(rows // 2)
    tiles = rows // tile
    middle = tiles // 2
    blocks = width // block
    depth = blocks // labels
    low = labels // 2
    size = block + 16

    def body(spot_ref, g_ref, r_ref, h_ref, oa_ref, ob_ref, gain_ref, a_ref, w_ref, *refs):
        gh_ref, ga_ref, lo_ref, hi_ref, acc, gains, all_blocks, sem = refs[len(deps) :]
        t = pl.program_id(0)
        h = h_ref[...]
        g = g_ref[...].astype(F32) + r_ref[...].astype(F32)
        dz = jnp.where(t < middle, oa_ref[...], ob_ref[...]).astype(F32)
        inv = rms_scale(h)
        scaled = g * gain_ref[...]
        grad = dz + inv * scaled - h * (
            inv * inv * inv * jnp.mean(scaled * h, axis=-1, keepdims=True)
        )

        @pl.when(t < middle)
        def _():
            gh_ref[...] = grad

        branch = grad.astype(BF)
        ga_ref[...] = nn(branch, w_ref[...]).astype(BF)
        part = tn(branch, a_ref[...])
        gain_part = jnp.sum(g * h * inv, axis=0, keepdims=True)

        @pl.when(t == 0)
        def _():
            acc[...] = part
            gains[...] = gain_part

        @pl.when(t > 0)
        def _():
            acc[...] += part
            gains[...] += gain_part

        @pl.when(t == tiles - 1)
        def _():
            all_blocks[:, block:] = jnp.zeros((blocks, 16, half), BF)
            for i in range(blocks):
                all_blocks[i, :block] = acc[i * block : (i + 1) * block].astype(BF)
                all_blocks[i, block : block + 1, :block] = gains[
                    :, i * block : (i + 1) * block
                ].astype(BF)
            copies = []
            for m in range(labels):
                out = lo_ref if m < low else hi_ref
                for d in range(depth):
                    i = m * depth + d
                    copies.append(
                        pltpu.make_async_copy(
                            all_blocks.at[spot_ref[i]], out.at[m % low, d], sem.at[i]
                        )
                    )
            for c in copies:
                c.start()
            for c in copies:
                c.wait()

    def rows_of(width, shift=0):
        return pl.BlockSpec((tile, width), lambda t: ((t + shift) % tiles, 0))

    def whole(a):
        return pl.BlockSpec(a.shape, lambda t: (0, 0))

    part = jax.ShapeDtypeStruct((low, depth, size, half), BF)
    first = pl.BlockSpec((tile, width), lambda t: (jnp.minimum(t, middle - 1), 0))
    second = pl.BlockSpec((tile, width), lambda t: (jnp.maximum(t - middle, 0), 0))
    return pl.pallas_call(
        body,
        out_shape=(
            jax.ShapeDtypeStruct((rows // 2, width), F32),
            jax.ShapeDtypeStruct((rows, half), BF),
            part,
            part,
        ),
        grid=(tiles,),
        in_specs=[
            in_smem(),
            rows_of(width),
            rows_of(width, middle),
            rows_of(width),
            first,
            second,
            whole(gain),
            rows_of(half),
            whole(out_mine),
        ]
        + [anywhere()] * len(deps),
        out_specs=[first, rows_of(half), anywhere(), anywhere()],
        scratch_shapes=[
            pltpu.VMEM((width, half), F32),
            pltpu.VMEM((1, width), F32),
            pltpu.VMEM((blocks, size, half), BF),
            pltpu.SemaphoreType.DMA((blocks,)),
        ],
        compiler_params=params(VMEM),
        cost_estimate=cost(4 * rows * width * half, 20e6),
    )(spots, grad_nt, grad_nt_other, hidden, og_own, og_other, gain, attended, out_mine, *deps)


def projection_grads(spots, xhat, grads, block, labels, deps=()):
    rows, width = xhat.shape
    count = len(grads)
    half = grads[0].shape[1]
    blocks = width // block
    depth = blocks // labels
    low = labels // 2

    def body(spot_ref, x_ref, *refs):
        ins = refs[:count]
        lo_ref, hi_ref, out, sem = refs[count + len(deps) :]
        x_t = x_ref[...].T
        copies = []
        for k in range(count):
            out[k] = nn(x_t, ins[k][...]).astype(BF)
            for m in range(labels):
                to = lo_ref if m < low else hi_ref
                for d in range(depth):
                    i = m * depth + d
                    start = pl.multiple_of(spot_ref[i] * block, block)
                    copies.append(
                        pltpu.make_async_copy(
                            out.at[k, pl.ds(start, block)],
                            to.at[m % low, d, pl.ds(k * block, block)],
                            sem.at[k, i],
                        )
                    )
                    copies[-1].start()
        for c in copies:
            c.wait()

    part = jax.ShapeDtypeStruct((low, depth, count * block, half), BF)
    return pl.pallas_call(
        body,
        out_shape=(part, part),
        in_specs=[in_smem()] + [in_vmem()] * (1 + count) + [anywhere()] * len(deps),
        out_specs=[anywhere()] * 2,
        scratch_shapes=[
            pltpu.VMEM((count, width, half), BF),
            pltpu.SemaphoreType.DMA((count, blocks)),
        ],
        compiler_params=params(VMEM),
        cost_estimate=cost(2 * count * rows * width * half, 8e6),
    )(spots, xhat, *grads, *deps)


def rows_grad(grads, w_all, deps=()):
    rows, half = grads[0].shape
    width = w_all.shape[1]
    tile = tile_of(rows // 2)
    tiles = rows // tile
    middle = tiles // 2

    def body(a_ref, b_ref, c_ref, w_ref, *refs):
        own_ref, other_ref = refs[len(deps) :]
        t = pl.program_id(0)
        y = nt(a_ref[...], w_ref[0]) + nt(b_ref[...], w_ref[1]) + nt(c_ref[...], w_ref[2])

        @pl.when(t < middle)
        def _():
            other_ref[...] = y.astype(BF)

        @pl.when(t >= middle)
        def _():
            own_ref[...] = y

    rows_in = pl.BlockSpec((tile, half), lambda t: ((t + middle) % tiles, 0))
    return pl.pallas_call(
        body,
        out_shape=(
            jax.ShapeDtypeStruct((rows // 2, width), F32),
            jax.ShapeDtypeStruct((rows // 2, width), BF),
        ),
        grid=(tiles,),
        in_specs=[rows_in] * 3
        + [pl.BlockSpec((3, width, half), lambda t: (0, 0, 0))]
        + [anywhere()] * len(deps),
        out_specs=[
            pl.BlockSpec((tile, width), lambda t: (jnp.maximum(t - middle, 0), 0)),
            pl.BlockSpec((tile, width), lambda t: (jnp.minimum(t, middle - 1), 0)),
        ],
        compiler_params=params(VMEM),
        cost_estimate=cost(6 * rows * width * half, 8e6),
    )(*grads, w_all, *deps)


class Grid:
    def __init__(self):
        self.depth = lax.axis_size(NARROW)
        self.wide = lax.axis_size(WIDE)
        self.plane = self.wide // 2
        self.bits = self.plane.bit_length() - 1
        place = lax.axis_index(WIDE)
        self.core = place % 2
        self.chip = place // 2
        self.level = lax.axis_index(NARROW)

    def flip(self, label):
        return sum(((label >> b) & 1) << (self.bits - 1 - b) for b in range(self.bits))

    def chip_of(self, label):
        return self.chip ^ jnp.where(self.core == 0, label, self.flip(label))

    def label_of(self, chip):
        return jnp.where(self.core == 0, self.chip ^ chip, self.flip(self.chip ^ chip))

    def other(self, array):
        return lax.ppermute(array, WIDE, [(i, i ^ 1) for i in range(self.wide)])

    def hop(self, array, bit):
        pairs = []
        for i in range(self.wide):
            step = bit if i % 2 == 0 else self.bits - 1 - bit
            pairs.append((i, i ^ (2 << step)))
        return lax.ppermute(array, WIDE, pairs)

    def lift(self, array, distance):
        return lax.ppermute(array, NARROW, [(i, i ^ distance) for i in range(self.depth)])

    def lifts(self, block, first=None, wait=None):
        out = [block]
        for d in range(1, self.depth):
            low = d & -d
            if d <= 2 and first is not None:
                out.append(first[d - 1])
                continue
            source = out[d ^ low]
            if wait is not None and d != low:
                source = tie(source, wait)
            out.append(self.lift(source, low))
        return out

    def spots(self):
        return jnp.stack(
            [
                (self.level ^ d) * self.plane + self.chip_of(label)
                for label in range(self.plane)
                for d in range(self.depth)
            ]
        ).astype(jnp.int32)

    def spread(self, levels, first=None, wait=None):
        parts = [levels]
        for label in range(1, self.plane):
            top = label.bit_length() - 1
            source = parts[label ^ (1 << top)]
            if first is not None and label in (1, 1 << (self.bits - 1)):
                parts.append(first[0] if label == 1 else first[1])
                continue
            if wait is not None and source is not levels:
                source = tie(source, wait)
            parts.append(self.hop(source, top))
        return parts

    def fold(self, low, high, waits=()):
        steps = []
        for bit in range(self.bits - 1, -1, -1):
            if len(steps) < len(waits) and waits[len(steps)] is not None:
                high = tie(high, waits[len(steps)])
            total = (low.astype(F32) + self.hop(high, bit).astype(F32)).astype(BF)
            low, high = total[: 1 << bit >> 1], total[1 << bit >> 1 :]
            steps.append(total)
        return steps[:-1] + [steps[-1][0]]

    def drop(self, blocks, first):
        blocks = [b.astype(F32) for b in blocks]
        bit = 1
        while bit < self.depth:
            for d in range(bit, self.depth, 2 * bit):
                came = first if d == 1 else self.lift(blocks[d].astype(BF), bit)
                blocks[d ^ bit] = blocks[d ^ bit] + came.astype(F32)
            bit *= 2
        return blocks[0]

    def drop_all(self, blocks):
        bit = 1
        while bit < self.depth:
            pairs = blocks.reshape((-1, 2) + blocks.shape[1:])
            came = self.lift(pairs[:, 1], bit).astype(F32)
            total = pairs[:, 0].astype(F32) + came
            bit *= 2
            blocks = total.astype(BF) if bit < self.depth else total
        return blocks[0]


def tie(array, *deps):
    return lax.optimization_barrier((array,) + deps)[0]


def on_device(
    layer_in,
    first_values,
    out_grad,
    seq_group,
    short_split,
    attn_gain,
    mlp_gain,
    w_query,
    w_key,
    w_value,
    w_out,
    w_gate,
    w_up,
    w_down,
):
    grid = Grid()
    core = grid.core
    rows, width = layer_in.shape
    half = width // 2
    heads = half // HEAD_DIM
    shard = w_query.shape[0]
    block = 2 * shard

    def pick(first, second):
        return jnp.where(core == 0, first, second)

    split_own = jnp.where(seq_group[0] == 0, rows, short_split[0])
    gain_col = attn_gain.astype(F32)[:, None]
    w4 = [(gain_col * w.astype(F32)).astype(BF) for w in (w_query, w_key, w_value)] + [w_out.T]
    spare = jnp.zeros((16, half), BF).at[0, :shard].set(mlp_gain)
    spare = spare.at[1, :2].set(jnp.stack([split_own // 256, split_own % 256]).astype(BF))
    mine = jnp.concatenate([pick(w[:, :half], w[:, half:]) for w in w4] + [spare])
    came = grid.other(
        jnp.concatenate([pick(w[:, half:], w[:, :half]) for w in w4] + [spare])
    )
    split_other = came[4 * shard + 1, :2].astype(jnp.int32)
    split_other = split_other[0] * 256 + split_other[1]
    own_block = assemble(core.reshape(1).astype(jnp.int32), mine, came, shard)

    ff3 = jnp.stack([w_gate.T, w_up.T, w_down])
    units = ff3.shape[1] // 2
    cols = ff3.shape[2]
    ff_mine = pick(ff3[:, :units], ff3[:, units:])
    ff_came = grid.other(pick(ff3[:, units:], ff3[:, :units]))
    ff_block = pick(
        jnp.concatenate([ff_mine, ff_came], 2), jnp.concatenate([ff_came, ff_mine], 2)
    )

    fv_left, fv_right = first_values[:, :half], first_values[:, half:]
    sent = jnp.concatenate([layer_in, pick(fv_right, fv_left)], 1)
    got = grid.other(sent)
    xb2 = jnp.concatenate([layer_in, got[:, :width]])
    x2 = xb2.astype(F32)
    fv2 = jnp.concatenate([pick(fv_left, fv_right), got[:, width:]])

    own_block = tie(own_block, got, ff_came)
    near_one = grid.hop(own_block, 0), grid.hop(own_block, grid.bits - 1)
    levels = grid.lifts(own_block)
    ff_own_block = tie(ff_block, *near_one)
    ff_own_one = grid.hop(ff_own_block, 0), grid.hop(ff_own_block, grid.bits - 1)
    level_blocks = tie(jnp.stack(levels[1:]), *near_one, *ff_own_one)
    ff_block_later = tie(ff_block, level_blocks)
    ff_first = grid.lift(ff_block_later, 1)
    far = grid.spread(level_blocks, wait=ff_first)
    near = grid.spread(own_block, first=near_one, wait=far[1])
    ff_own = grid.spread(ff_own_block, first=ff_own_one, wait=far[-1])
    ff_second = grid.lift(ff_block_later, 2)
    chips = jnp.stack([grid.chip_of(m) for m in range(grid.plane)]).astype(jnp.int32)
    spots = grid.spots()

    row_index = jnp.arange(rows, dtype=jnp.int32)
    splits = jnp.stack([split_own, split_other])
    lane = jnp.arange(128) % HEAD_DIM
    frequency = jnp.exp(
        (lane % (HEAD_DIM // 2)).astype(F32) * (-2.0 * math.log(10000.0) / HEAD_DIM)
    )
    second = row_index[None, :] >= splits[:, None]
    position = jnp.where(second, row_index[None, :] - splits[:, None], row_index[None, :])
    turned = position.astype(F32).reshape(-1)[:, None] * frequency[None, :]
    cos = jnp.cos(turned)
    sin = jnp.sin(turned) * jnp.where(lane < HEAD_DIM // 2, -1.0, 1.0)

    inv1 = rms_scale(x2)
    xhat = (x2 * inv1).astype(BF)
    queries, keys, values, w_all, out_mine, gains = project_rows(
        xhat, fv2, cos, sin, near, far, spots, block
    )
    out_other = grid.other(out_mine)
    og_other = grid.other(tie(out_grad, queries))
    ff_one = grid.spread(tie(ff_first, far[-1]), wait=queries)
    ff_levels = grid.lifts(ff_block_later, first=(ff_first, ff_second), wait=queries)
    ff_far = grid.spread(tie(jnp.concatenate(ff_levels[2:], 1), ff_one[3]))
    attended, weights = attend(
        splits, queries, keys, values, deps=[ff_own[3], ff_one[1], ff_one[2], ff_levels[2]]
    )
    att_other = grid.other(attended)

    gain_mlp = gains.reshape(-1, 16, half)[:, :2, :shard].reshape(1, width).astype(F32)
    hidden, normed_two = out_and_norm(
        xb2, attended, att_other, out_mine, out_other, gain_mlp
    )

    def feed(parts, before=None, deps=()):
        if parts[0].shape[-1] % 128 == 0:
            return feed_forward(chips, normed_two, out_grad, og_other, parts, before, deps)
        stacked = jnp.stack(parts)
        whole = jnp.concatenate([stacked[grid.label_of(b)] for b in range(grid.plane)], axis=-1)
        sums, grads = feed_forward(
            chips, normed_two, out_grad, og_other, [whole], before, deps
        )
        grads = grads[0][0].reshape(whole.shape[:-1] + (grid.plane, 2 * cols))
        grads = [grads[..., grid.chip_of(m), :] for m in range(grid.plane)]
        middle = grid.plane // 2
        return sums, [jnp.stack(grads[:middle]), jnp.stack(grads[middle:])]

    sums, grads_a = feed(ff_own, deps=[ff_far[1], ff_far[2]])
    sums, grads_b = feed(ff_one, before=sums, deps=[ff_far[3]])
    fold_a = grid.fold(*grads_a, waits=[None, sums[2]])
    sums, grads_c = feed(ff_far, before=sums, deps=[fold_a[0]])
    fold_b = grid.fold(*grads_b, waits=[None, sums[2]])
    branch, branch_sent, grad_nt = sums
    grad_nt_other = grid.other(tie(grad_nt, fold_a[-1]))
    grad_hidden, grad_att, out_low, out_high = norm_two_back(
        spots, grad_nt, grad_nt_other, hidden, out_grad, og_other, gain_mlp,
        attended, out_mine, block, grid.plane,
    )
    branch_other = grid.other(tie(branch_sent, grad_att))
    layer_out = (hidden[:rows] + branch.astype(F32) + branch_other.astype(F32)).astype(BF)

    pairs = half // 256
    back_one = attend_back(
        queries, keys, values, weights, grad_att, cos, sin, 0, pairs, deps=[fold_b[-1]]
    )
    out_fold = grid.fold(out_low, out_high, waits=[None, back_one[0]])
    fold_c = grid.fold(*grads_c, waits=[None, back_one[0]])
    lifted = grid.lift(tie(fold_b[-1], grad_att), 1)
    back_two = attend_back(
        queries, keys, values, weights, grad_att, cos, sin, pairs, pairs,
        deps=[fold_c[0], lifted, out_fold[0], back_one[0]],
    )
    grad_qp, grad_kp, values_half = (
        jnp.concatenate(pair, 1) for pair in zip(back_one, back_two)
    )
    grad_vp = values_half.astype(BF)
    v_keep = values_half[:rows]
    v_got = grid.other(grad_vp[rows:]).astype(F32)
    values_grad = pick(
        jnp.concatenate([v_keep, v_got], 1), jnp.concatenate([v_got, v_keep], 1)
    )
    proj = (grad_qp, grad_kp, grad_vp)
    qkv_low, qkv_high = projection_grads(
        spots, xhat, proj, block, grid.plane, deps=[fold_c[-1], out_fold[-1]]
    )
    qkv_total = grid.drop_all(grid.fold(qkv_low, qkv_high)[-1]).reshape(3, block, half)
    scaled_own, scaled_sent = rows_grad(proj, w_all, deps=[qkv_low])
    out_total = grid.drop_all(out_fold[-1])
    rest = [fold_c[-1][:, i * units : (i + 1) * units] for i in range(grid.depth - 2)]
    total = grid.drop([fold_a[-1], fold_b[-1]] + rest, first=lifted)
    keep = pick(total[:, :, :cols], total[:, :, cols:])
    got = grid.other(pick(total[:, :, cols:], total[:, :, :cols]).astype(BF)).astype(F32)
    ff_grads = pick(jnp.concatenate([keep, got], 1), jnp.concatenate([got, keep], 1))
    scaled_one = scaled_own + grid.other(scaled_sent).astype(F32)
    x1, i1 = x2[:rows], inv1[:rows]
    in_grad = (
        grad_hidden
        + i1 * scaled_one
        - x1 * (i1 * i1 * i1) * jnp.mean(scaled_one * x1, axis=-1, keepdims=True)
    )

    def own_rows(total):
        keep = pick(total[..., :shard, :], total[..., shard:, :])
        got = grid.other(pick(total[..., shard:, :], total[..., :shard, :]).astype(BF))
        got = got.astype(F32)
        return pick(jnp.concatenate([keep, got], -1), jnp.concatenate([got, keep], -1))

    plain = own_rows(qkv_total)
    attn_gain_grad = sum(
        jnp.sum(plain[k] * w.astype(F32), axis=-1)
        for k, w in enumerate((w_query, w_key, w_value))
    )
    out_proj_grad = own_rows(out_total[:block]).T
    gain_total = out_total[block]
    mlp_gain_grad = pick(gain_total[:shard], gain_total[shard : 2 * shard])
    return (
        layer_out,
        in_grad,
        values_grad,
        attn_gain_grad,
        mlp_gain_grad,
        gain_col * plain[0],
        gain_col * plain[1],
        gain_col * plain[2],
        out_proj_grad,
        ff_grads[0].T,
        ff_grads[1].T,
        ff_grads[2],
    )


def solution(mesh):
    rows = P((NARROW, WIDE), None)
    line = P((NARROW, WIDE))
    lanes = P(None, (NARROW, WIDE))
    return jax.shard_map(
        on_device,
        mesh=mesh,
        in_specs=(
            (rows,) * 3 + (line,) * 4 + (rows,) * 3
            + (lanes, P(WIDE, NARROW), P(WIDE, NARROW), P(NARROW, WIDE))
        ),
        out_specs=(
            (rows,) * 3 + (line,) * 2 + (rows,) * 3
            + (lanes, P(WIDE, NARROW), P(WIDE, NARROW), P(NARROW, WIDE))
        ),
        check_vma=False,
    )
```

```python
import math

import jax
import jax.numpy as jnp
from jax import lax
from jax.experimental import pallas as pl
from jax.experimental.pallas import tpu as pltpu
from jax.sharding import PartitionSpec as P

HEAD_DIM = 64
EPS = 1e-06
BF = jnp.bfloat16
F32 = jnp.float32
NARROW, WIDE = "narrow", "wide"
VMEM = 60
HEADS_AT_ONCE = 4


def dot(left, right, dims):
    return lax.dot_general(left, right, (dims, ((), ())), preferred_element_type=F32)


def nn(left, right):
    return dot(left, right, ((1,), (0,)))


def nt(left, right):
    return dot(left, right, ((1,), (1,)))


def tn(left, right):
    return dot(left, right, ((0,), (0,)))


def rms_scale(values):
    return lax.rsqrt(jnp.mean(values * values, axis=-1, keepdims=True) + EPS)


def tile_of(rows):
    return min(256, rows)


def anywhere():
    return pl.BlockSpec(memory_space=pl.ANY)


def in_smem():
    return pl.BlockSpec(memory_space=pltpu.SMEM)


def in_vmem():
    return pl.BlockSpec(memory_space=pltpu.VMEM)


def params(mib):
    return pltpu.CompilerParams(vmem_limit_bytes=mib * 1024 * 1024)


def cost(flops, moved):
    return pl.CostEstimate(
        flops=int(2 * flops), bytes_accessed=int(moved), transcendentals=0
    )


def turn(v, cos, sin):
    lane = lax.broadcasted_iota(jnp.int32, v.shape, 1)
    swapped = jnp.where(
        lane % HEAD_DIM < HEAD_DIM // 2,
        pltpu.roll(v, 128 - HEAD_DIM // 2, 1),
        pltpu.roll(v, HEAD_DIM // 2, 1),
    )
    return v * cos + swapped * sin


def assemble(core, mine, came, shard):
    half = mine.shape[1]

    def body(core_ref, mine_ref, came_ref, out_ref):
        own, other = mine_ref[...].astype(F32), came_ref[...].astype(F32)
        first = core_ref[0] == 0
        lower, upper = jnp.where(first, own, other), jnp.where(first, other, own)
        for k in range(4):
            at = slice(k * shard, (k + 1) * shard)
            pair = jnp.concatenate([lower[at], upper[at]], 0)
            out_ref[2 * k * shard : 2 * (k + 1) * shard] = pair.astype(BF)
        row = lax.broadcasted_iota(jnp.int32, (16, half), 0)
        spare = jnp.where(row == 0, lower[4 * shard : 4 * shard + 1], upper[4 * shard : 4 * shard + 1])
        out_ref[8 * shard :] = spare.astype(BF)

    return pl.pallas_call(
        body,
        out_shape=jax.ShapeDtypeStruct((8 * shard + 16, half), BF),
        in_specs=[in_smem(), in_vmem(), in_vmem()],
        out_specs=in_vmem(),
        compiler_params=params(VMEM),
    )(core, mine, came)


def project_rows(xhat, fv2, cos, sin, near, far, spots, block, deps=()):
    count, depth = len(near), far[0].shape[0] + 1
    blocks = count * depth
    rows, width = xhat.shape
    half = fv2.shape[1]
    tile = min(512, rows)

    def body(spot_ref, x_hbm, fv_hbm, cos_hbm, sin_hbm, *refs):
        refs = list(refs)
        sources = refs[: 2 * count]
        refs = refs[2 * count + len(deps) :]
        outs, w_out, wo_out, g_out = refs[:3], refs[3], refs[4], refs[5]
        x_ref, fv_ref, cos_ref, sin_ref, w_ref, wo_ref, g_ref, y_ref, sem, isem, osem = refs[6:]

        def weights(k):
            copies = []
            for m in range(count):
                for d in range(depth):
                    i = m * depth + d
                    source = sources[m] if d == 0 else sources[count + m].at[d - 1]
                    size = block if k < 4 else 16
                    to = pl.ds(pl.multiple_of(spot_ref[i] * size, size), size)
                    out = w_ref.at[k, to] if k < 3 else (wo_ref if k == 3 else g_ref).at[to]
                    copies.append(
                        pltpu.make_async_copy(source.at[pl.ds(k * block, size)], out, sem.at[k, i])
                    )
                    copies[-1].start()
            return copies

        ins = [
            pltpu.make_async_copy(a, b, isem.at[n])
            for n, (a, b) in enumerate(
                ((x_hbm, x_ref), (cos_hbm, cos_ref), (sin_hbm, sin_ref), (fv_hbm, fv_ref))
            )
        ]
        ins[0].start()
        arriving = [weights(0)]
        for c in ins[1:]:
            c.start()
        arriving += [weights(k) for k in range(1, 5)]
        for c in ins[:3]:
            c.wait()
        sends = []

        def send(source, to, n):
            sends.append(pltpu.make_async_copy(source, to, osem.at[n]))
            sends[-1].start()

        for k in range(3):
            for c in arriving[k]:
                c.wait()
            send(w_ref.at[k], w_out.at[k], k)
            if k == 2:
                ins[3].wait()
            for t in range(rows // tile):
                at = slice(t * tile, (t + 1) * tile)
                y = nn(x_ref[at], w_ref[k])
                if k == 2:
                    y_ref[k, at] = (0.5 * y + 0.5 * fv_ref[at].astype(F32)).astype(BF)
                else:
                    factor = HEAD_DIM ** (-0.5) if k == 0 else 1.0
                    cos_t, sin_t = cos_ref[at] * factor, sin_ref[at] * factor
                    for g in range(half // 128):
                        lanes = slice(g * 128, g * 128 + 128)
                        y_ref[k, at, lanes] = turn(y[:, lanes], cos_t, sin_t).astype(BF)
            send(y_ref.at[k], outs[k], 3 + k)
        for k, (source, to) in ((3, (wo_ref, wo_out)), (4, (g_ref, g_out))):
            for c in arriving[k]:
                c.wait()
            send(source, to, 3 + k)
        for c in sends:
            c.wait()

    shape = jax.ShapeDtypeStruct((rows, half), BF)
    return pl.pallas_call(
        body,
        out_shape=(
            shape,
            shape,
            shape,
            jax.ShapeDtypeStruct((3, width, half), BF),
            jax.ShapeDtypeStruct((width, half), BF),
            jax.ShapeDtypeStruct((16 * blocks, half), BF),
        ),
        in_specs=[in_smem()] + [anywhere()] * (4 + 2 * count + len(deps)),
        out_specs=[anywhere()] * 6,
        scratch_shapes=[
            pltpu.VMEM((rows, width), BF),
            pltpu.VMEM((rows, half), BF),
            pltpu.VMEM((rows, 128), F32),
            pltpu.VMEM((rows, 128), F32),
            pltpu.VMEM((3, width, half), BF),
            pltpu.VMEM((width, half), BF),
            pltpu.VMEM((16 * blocks, half), BF),
            pltpu.VMEM((3, rows, half), BF),
            pltpu.SemaphoreType.DMA((5, blocks)),
            pltpu.SemaphoreType.DMA((4,)),
            pltpu.SemaphoreType.DMA((8,)),
        ],
        compiler_params=params(VMEM),
        cost_estimate=cost(6 * rows * width * half, 12e6),
    )(spots, xhat, fv2, cos, sin, *near, *far, *deps)


def query_blocks(rows):
    step = tile_of(rows)
    return [(s, step, s + step) for s in range(0, rows, step)]


def attend(splits, queries, keys, values, deps=()):
    rows2, half = queries.shape
    rows = rows2 // 2
    group = min(HEADS_AT_ONCE, half // HEAD_DIM)
    lanes = group * HEAD_DIM
    groups = half // lanes

    def body(split_ref, q_ref, k_ref, v_ref, *refs):
        o_ref, p_ref, bias, v_t = refs[len(deps) :]
        slot = pl.program_id(0)

        @pl.when(pl.program_id(1) == 0)
        def _():
            split = split_ref[slot]
            key = lax.broadcasted_iota(jnp.int32, (rows, rows), 0)
            query = lax.broadcasted_iota(jnp.int32, (rows, rows), 1)
            low = jnp.where(query >= split, split, 0)
            bias[...] = jnp.where((key <= query) & (key >= low), 0.0, -1e30)

        v_t[...] = v_ref[...].T
        lane = lax.broadcasted_iota(jnp.int32, (rows, 128), 1)
        feature = lax.broadcasted_iota(jnp.int32, (128, 1), 0)
        chains = [
            (block, h) for block in reversed(query_blocks(rows)) for h in range(group)
        ]

        def scores(chain):
            (start, count, key_end), h = chain
            at = slice(start, start + count)
            pair = slice(h // 2 * 128, h // 2 * 128 + 128)
            in_head = (lane[:key_end] < 64) if h % 2 == 0 else (lane[:key_end] >= 64)
            k = jnp.where(in_head, k_ref[:key_end, pair], 0)
            return nt(k, q_ref[at, pair]) + bias[:key_end, at]

        ahead = scores(chains[0])
        outs = []
        for i, chain in enumerate(chains):
            (start, count, key_end), h = chain
            at = slice(start, start + count)
            pair = slice(h // 2 * 128, h // 2 * 128 + 128)
            s = ahead
            if i + 1 < len(chains):
                ahead = scores(chains[i + 1])
            e = jnp.exp(s - jnp.max(s, axis=0, keepdims=True))
            p = (e * (1.0 / jnp.sum(e, axis=0, keepdims=True))).astype(BF)
            p_ref[h, :key_end, at] = p
            outs.append(nn(v_t[pair, :key_end], p))
            if h % 2 == 1:
                o = jnp.where(feature < 64, outs[-2], outs[-1])
                o_ref[at, pair] = o.astype(BF).T

    spec = pl.BlockSpec((rows, lanes), lambda s, p, *_: (s, p))
    return pl.pallas_call(
        body,
        out_shape=(
            jax.ShapeDtypeStruct((rows2, half), BF),
            jax.ShapeDtypeStruct((2 * half // HEAD_DIM, rows, rows), BF),
        ),
        grid_spec=pltpu.PrefetchScalarGridSpec(
            num_scalar_prefetch=1,
            grid=(2, groups),
            in_specs=[spec] * 3 + [anywhere()] * len(deps),
            out_specs=[
                spec,
                pl.BlockSpec((group, rows, rows), lambda s, p, *_: (s * groups + p, 0, 0)),
            ],
            scratch_shapes=[pltpu.VMEM((rows, rows), F32), pltpu.VMEM((lanes, rows), BF)],
        ),
        compiler_params=params(VMEM),
        cost_estimate=cost(16 * rows * rows * half, 12e6),
    )(splits, queries, keys, values, *deps)


def attend_back(queries, keys, values, weights, grad_att, cos, sin, start, pairs, deps=()):
    rows2, half = queries.shape
    rows = rows2 // 2
    lanes = 128 * pairs
    group = 2 * pairs
    groups = half // lanes
    blocks = query_blocks(rows)

    def body(q_ref, k_ref, v_ref, p_ref, ga_ref, cos_ref, sin_ref, *refs):
        gq_ref, gk_ref, gv_ref, own_ref, k_t, gs_sc = refs[len(deps) :]
        k_t[...] = k_ref[...].T
        lane = lax.broadcasted_iota(jnp.int32, (rows, 128), 1)
        feature = lax.broadcasted_iota(jnp.int32, (128, 1), 0)
        chains = [(h, block) for h in range(group) for block in blocks]

        def pair_of(h):
            return slice(h // 2 * 128, h // 2 * 128 + 128)

        def grad_probs(chain):
            h, (first, count, key_end) = chain
            in_head = (lane[:key_end] < 64) if h % 2 == 0 else (lane[:key_end] >= 64)
            v = jnp.where(in_head, v_ref[:key_end, pair_of(h)], 0)
            return nt(v, ga_ref[first : first + count, pair_of(h)])

        ahead = grad_probs(chains[0])
        gq, gk, gv = {}, {}, {}
        for i, (h, (first, count, key_end)) in enumerate(chains):
            at, pair = slice(first, first + count), pair_of(h)
            gp = ahead
            if i + 1 < len(chains):
                ahead = grad_probs(chains[i + 1])
            pf = p_ref[h, :key_end, at].astype(F32)
            delta = jnp.sum(gp * pf, axis=0, keepdims=True)
            gs = (pf * (gp - delta)).astype(BF)
            gs_sc[h % 2, :key_end, at] = gs
            gq[h, first] = nn(k_t[pair, :key_end], gs)
            if first + count < rows:
                continue
            for low, size, _ in blocks:
                mine = slice(low, low + size)
                gk[h, low] = nn(gs_sc[h % 2, mine, low:], q_ref[low:, pair])
                gv[h, low] = nn(p_ref[h, mine, low:], ga_ref[low:, pair])
            if h % 2 == 0:
                continue
            for low, size, _ in blocks:
                mine = slice(low, low + size)
                c, s = cos_ref[mine], -sin_ref[mine]
                both = jnp.where(feature < 64, gq[h - 1, low], gq[h, low])
                gq_ref[mine, pair] = turn((both * HEAD_DIM ** (-0.5)).T, c, s).astype(BF)
                both = jnp.where(lane[:size] < 64, gk[h - 1, low], gk[h, low])
                gk_ref[mine, pair] = turn(both, c, s).astype(BF)
                both = 0.5 * jnp.where(lane[:size] < 64, gv[h - 1, low], gv[h, low])
                gv_ref[mine, pair] = both.astype(BF)

                @pl.when(pl.program_id(0) == 0)
                def _():
                    own_ref[mine, pair] = both

    spec = pl.BlockSpec((rows, lanes), lambda s: (s, start))
    out = pl.BlockSpec((rows, lanes), lambda s: (s, 0))
    table = pl.BlockSpec((rows, 128), lambda s: (s, 0))
    shape = jax.ShapeDtypeStruct((rows2, lanes), BF)
    return pl.pallas_call(
        body,
        out_shape=(shape, shape, shape, jax.ShapeDtypeStruct((rows, lanes), F32)),
        grid=(2,),
        in_specs=[spec] * 3
        + [pl.BlockSpec((group, rows, rows), lambda s: (s * groups + start, 0, 0))]
        + [spec, table, table]
        + [anywhere()] * len(deps),
        out_specs=[out] * 3 + [pl.BlockSpec((rows, lanes), lambda s: (0, 0))],
        scratch_shapes=[pltpu.VMEM((lanes, rows), BF), pltpu.VMEM((2, rows, rows), BF)],
        compiler_params=params(VMEM),
        cost_estimate=cost(32 * rows * rows * lanes, 8e6),
    )(queries, keys, values, weights, grad_att, cos, sin, *deps)


def feed_forward(chips, normed_two, og_own, og_other, parts, before=None, deps=()):
    levels, count = len(parts), len(parts[0])
    _, each, lanes = parts[0][0].shape
    units = levels * each
    flat = [a for level in parts for a in level]
    rows, width = normed_two.shape
    tile = min(512, rows // 2)
    tiles = rows // tile
    more = 0 if before is None else 3
    groups = min(2, count)
    low = count // groups

    def body(chip_ref, nt_hbm, og_first, og_second, *refs):
        ins, refs = refs[: len(flat)], refs[len(flat) :]
        olds = refs[:more]
        refs = refs[more + len(deps) :]
        br_outs, gn_hbm, outs = refs[:2], refs[2], refs[3 : 3 + groups]
        x_all, o_all, w, act, gg, gu, ob, br, gn, rsem, wsem, osem, psem = refs[3 + groups :]

        def lanes_at(m):
            if count == 1:
                return slice(None)
            return pl.ds(pl.multiple_of(chip_ref[m] * lanes, lanes), lanes)

        def rows_at(t):
            return pl.ds(t * tile, tile)

        row_in, weight_in, old_in = [], [], []
        per_core = tiles // 2

        def part_of(pair, t):
            return pair[t // per_core].at[rows_at(t % per_core)]

        for t in range(tiles):
            row_in.append((
                pltpu.make_async_copy(nt_hbm.at[rows_at(t)], x_all.at[rows_at(t)], rsem.at[0, t]),
                pltpu.make_async_copy(
                    part_of((og_first, og_second), t), o_all.at[rows_at(t)], rsem.at[1, t]
                ),
            ))
            old_in.append([])
            if more:
                old_in[t].append(
                    pltpu.make_async_copy(part_of(olds[:2], t), br.at[rows_at(t)], psem.at[0, t])
                )
                old_in[t].append(
                    pltpu.make_async_copy(olds[2].at[rows_at(t)], gn.at[rows_at(t)], psem.at[1, t])
                )
        for k in range(3):
            weight_in.append([
                pltpu.make_async_copy(
                    ins[v * count + m].at[k],
                    w.at[k, pl.ds(v * each, each), lanes_at(m)],
                    wsem.at[k, v * count + m],
                )
                for v in range(levels)
                for m in range(count)
            ])
        row_in[0][0].start()
        for k in range(3):
            for c in weight_in[k]:
                c.start()
            if k == 1:
                row_in[0][1].start()
        for t in range(1, tiles):
            row_in[t][0].start()
            row_in[t][1].start()
        for t in range(tiles):
            for c in old_in[t]:
                c.start()

        sends = []
        for t in range(tiles):
            at = rows_at(t)
            row_in[t][0].wait()
            x = x_all[at]
            if t == 0:
                for c in weight_in[0]:
                    c.wait()
            gate = nt(w[0], x)
            if t == 0:
                for c in weight_in[1]:
                    c.wait()
            up = nt(w[1], x)
            row_in[t][1].wait()
            if t == 0:
                for c in weight_in[2]:
                    c.wait()
            ga = nt(w[2], o_all[at])
            sig = jax.nn.sigmoid(gate)
            soft = gate * sig
            a = (soft * up).astype(BF)
            g = (ga * up * (sig + soft * (1.0 - sig))).astype(BF)
            u = (ga * soft).astype(BF)
            act[:, at] = a
            gg[:, at] = g
            gu[:, at] = u
            b = tn(a, w[2])
            n = tn(g, w[0]) + tn(u, w[1])
            if more:
                for c in old_in[t]:
                    c.wait()
                b = b + br[at].astype(F32)
                n = n + gn[at].astype(F32)
            br[at] = b.astype(BF)
            gn[at] = n.astype(BF)
            sends.append(pltpu.make_async_copy(br.at[at], part_of(br_outs, t), rsem.at[0, t]))
            sends.append(pltpu.make_async_copy(gn.at[at], gn_hbm.at[at], rsem.at[1, t]))
            sends[-2].start()
            sends[-1].start()

        for m in reversed(range(count)):
            at = lanes_at(m)
            x, o = x_all[:, at], o_all[:, at]
            for k, left, right in ((0, gg, x), (1, gu, x), (2, act, o)):
                ob[m, k] = nn(left[...], right).astype(BF)
            sends.append(pltpu.make_async_copy(ob.at[m], outs[m // low].at[m % low], osem.at[m]))
            sends[-1].start()
        for c in sends:
            c.wait()

    shape = jax.ShapeDtypeStruct((rows, width), BF)
    part_rows = jax.ShapeDtypeStruct((rows // 2, width), BF)
    part = jax.ShapeDtypeStruct((low, 3, units, lanes), BF)
    out = pl.pallas_call(
        body,
        out_shape=(part_rows, part_rows, shape) + (part,) * groups,
        in_specs=[in_smem()] + [anywhere()] * (3 + len(flat) + more + len(deps)),
        out_specs=[anywhere()] * (3 + groups),
        scratch_shapes=[
            pltpu.VMEM((rows, width), BF),
            pltpu.VMEM((rows, width), BF),
            pltpu.VMEM((3, units, width), BF),
            pltpu.VMEM((units, rows), BF),
            pltpu.VMEM((units, rows), BF),
            pltpu.VMEM((units, rows), BF),
            pltpu.VMEM((count, 3, units, lanes), BF),
            pltpu.VMEM((rows, width), BF),
            pltpu.VMEM((rows, width), BF),
            pltpu.SemaphoreType.DMA((2, tiles)),
            pltpu.SemaphoreType.DMA((3, len(flat))),
            pltpu.SemaphoreType.DMA((count,)),
            pltpu.SemaphoreType.DMA((2, tiles)),
        ],
        compiler_params=params(VMEM),
        cost_estimate=cost(18 * rows * width * units, 12e6),
    )(chips, normed_two, og_own, og_other, *flat, *(before or ()), *deps)
    return out[:3], list(out[3:])


def out_and_norm(x_own, x_other, attended, att_other, out_mine, out_other, gain, deps=()):
    rows, half = attended.shape
    width = x_own.shape[1]
    tile = tile_of(rows // 2)
    tiles = rows // tile
    middle = tiles // 2

    def body(xa_ref, xb_ref, a_ref, b_ref, wa_ref, wb_ref, gain_ref, *refs):
        h_ref, n_ref = refs[len(deps) :]
        x = jnp.where(pl.program_id(0) < middle, xa_ref[...], xb_ref[...])
        h = x.astype(F32) + nt(a_ref[...], wa_ref[...]) + nt(b_ref[...], wb_ref[...])
        h_ref[...] = h
        n_ref[...] = (h * rms_scale(h) * gain_ref[...]).astype(BF)

    def rows_of(width, shift=0):
        return pl.BlockSpec((tile, width), lambda t: ((t + shift) % tiles, 0))

    def whole(a):
        return pl.BlockSpec(a.shape, lambda t: (0, 0))

    return pl.pallas_call(
        body,
        out_shape=(
            jax.ShapeDtypeStruct((rows, width), F32),
            jax.ShapeDtypeStruct((rows, width), BF),
        ),
        grid=(tiles,),
        in_specs=[
            pl.BlockSpec((tile, width), lambda t: (jnp.minimum(t, middle - 1), 0)),
            pl.BlockSpec((tile, width), lambda t: (jnp.maximum(t - middle, 0), 0)),
            rows_of(half),
            rows_of(half, middle),
            whole(out_mine),
            whole(out_other),
            whole(gain),
        ]
        + [anywhere()] * len(deps),
        out_specs=[rows_of(width)] * 2,
        compiler_params=params(VMEM),
        cost_estimate=cost(4 * rows * width * half, 12e6),
    )(x_own, x_other, attended, att_other, out_mine, out_other, gain, *deps)


def norm_two_back(spots, grad_nt, grad_nt_other, hidden, og_own, og_other, gain, attended, out_mine, block, labels, deps=()):
    rows, width = hidden.shape
    half = attended.shape[1]
    tile = tile_of(rows // 2)
    tiles = rows // tile
    middle = tiles // 2
    blocks = width // block
    depth = blocks // labels
    low = labels // 2
    size = block + 16

    def body(spot_ref, g_ref, r_ref, h_ref, oa_ref, ob_ref, gain_ref, a_ref, w_ref, *refs):
        gh_ref, ga_ref, lo_ref, hi_ref, acc, gains, all_blocks, sem = refs[len(deps) :]
        t = pl.program_id(0)
        h = h_ref[...]
        g = g_ref[...].astype(F32) + r_ref[...].astype(F32)
        dz = jnp.where(t < middle, oa_ref[...], ob_ref[...]).astype(F32)
        inv = rms_scale(h)
        scaled = g * gain_ref[...]
        grad = dz + inv * scaled - h * (
            inv * inv * inv * jnp.mean(scaled * h, axis=-1, keepdims=True)
        )

        @pl.when(t < middle)
        def _():
            gh_ref[...] = grad

        branch = grad.astype(BF)
        ga_ref[...] = nn(branch, w_ref[...]).astype(BF)
        part = tn(branch, a_ref[...])
        gain_part = jnp.sum(g * h * inv, axis=0, keepdims=True)

        @pl.when(t == 0)
        def _():
            acc[...] = part
            gains[...] = gain_part

        @pl.when(t > 0)
        def _():
            acc[...] += part
            gains[...] += gain_part

        @pl.when(t == tiles - 1)
        def _():
            all_blocks[:, block:] = jnp.zeros((blocks, 16, half), BF)
            for i in range(blocks):
                all_blocks[i, :block] = acc[i * block : (i + 1) * block].astype(BF)
                all_blocks[i, block : block + 1, :block] = gains[
                    :, i * block : (i + 1) * block
                ].astype(BF)
            copies = []
            for m in range(labels):
                out = lo_ref if m < low else hi_ref
                for d in range(depth):
                    i = m * depth + d
                    copies.append(
                        pltpu.make_async_copy(
                            all_blocks.at[spot_ref[i]], out.at[m % low, d], sem.at[i]
                        )
                    )
            for c in copies:
                c.start()
            for c in copies:
                c.wait()

    def rows_of(width, shift=0):
        return pl.BlockSpec((tile, width), lambda t: ((t + shift) % tiles, 0))

    def whole(a):
        return pl.BlockSpec(a.shape, lambda t: (0, 0))

    part = jax.ShapeDtypeStruct((low, depth, size, half), BF)
    first = pl.BlockSpec((tile, width), lambda t: (jnp.minimum(t, middle - 1), 0))
    second = pl.BlockSpec((tile, width), lambda t: (jnp.maximum(t - middle, 0), 0))
    return pl.pallas_call(
        body,
        out_shape=(
            jax.ShapeDtypeStruct((rows // 2, width), F32),
            jax.ShapeDtypeStruct((rows, half), BF),
            part,
            part,
        ),
        grid=(tiles,),
        in_specs=[
            in_smem(),
            rows_of(width),
            rows_of(width, middle),
            rows_of(width),
            first,
            second,
            whole(gain),
            rows_of(half),
            whole(out_mine),
        ]
        + [anywhere()] * len(deps),
        out_specs=[first, rows_of(half), anywhere(), anywhere()],
        scratch_shapes=[
            pltpu.VMEM((width, half), F32),
            pltpu.VMEM((1, width), F32),
            pltpu.VMEM((blocks, size, half), BF),
            pltpu.SemaphoreType.DMA((blocks,)),
        ],
        compiler_params=params(VMEM),
        cost_estimate=cost(4 * rows * width * half, 20e6),
    )(spots, grad_nt, grad_nt_other, hidden, og_own, og_other, gain, attended, out_mine, *deps)


def projection_grads(spots, xhat, grads, block, labels, deps=()):
    rows, width = xhat.shape
    count = len(grads)
    half = grads[0].shape[1]
    blocks = width // block
    depth = blocks // labels
    low = labels // 2

    def body(spot_ref, x_ref, *refs):
        ins = refs[:count]
        lo_ref, hi_ref, out, sem = refs[count + len(deps) :]
        x_t = x_ref[...].T
        copies = []
        for k in range(count):
            out[k] = nn(x_t, ins[k][...]).astype(BF)
            for m in range(labels):
                to = lo_ref if m < low else hi_ref
                for d in range(depth):
                    i = m * depth + d
                    start = pl.multiple_of(spot_ref[i] * block, block)
                    copies.append(
                        pltpu.make_async_copy(
                            out.at[k, pl.ds(start, block)],
                            to.at[m % low, d, pl.ds(k * block, block)],
                            sem.at[k, i],
                        )
                    )
                    copies[-1].start()
        for c in copies:
            c.wait()

    part = jax.ShapeDtypeStruct((low, depth, count * block, half), BF)
    return pl.pallas_call(
        body,
        out_shape=(part, part),
        in_specs=[in_smem()] + [in_vmem()] * (1 + count) + [anywhere()] * len(deps),
        out_specs=[anywhere()] * 2,
        scratch_shapes=[
            pltpu.VMEM((count, width, half), BF),
            pltpu.SemaphoreType.DMA((count, blocks)),
        ],
        compiler_params=params(VMEM),
        cost_estimate=cost(2 * count * rows * width * half, 8e6),
    )(spots, xhat, *grads, *deps)


def rows_grad(grads, w_all, branch, deps=()):
    rows, lanes = grads[0][0].shape
    width, half = w_all.shape[1:]
    flat = [g for group in grads for g in group]
    tile = tile_of(rows // 2)
    tiles = rows // tile
    middle = tiles // 2

    def body(*refs):
        ins, w_ref, b_ref = refs[: len(flat)], refs[len(flat)], refs[len(flat) + 1]
        own_ref, other_ref = refs[len(flat) + 2 + len(deps) :]
        t = pl.program_id(0)
        y = None
        for k in range(3):
            g = jnp.concatenate([ins[3 * i + k][...] for i in range(len(grads))], 1)
            part = nt(g, w_ref[k])
            y = part if y is None else y + part

        @pl.when(t < middle)
        def _():
            other_ref[:, :width] = y.astype(BF)
            other_ref[:, width : 2 * width] = b_ref[...]
            for i in range(len(grads)):
                other_ref[:, 2 * width + i * lanes : 2 * width + (i + 1) * lanes] = ins[3 * i + 2][...]

        @pl.when(t >= middle)
        def _():
            own_ref[...] = y

    rows_in = pl.BlockSpec((tile, lanes), lambda t: ((t + middle) % tiles, 0))
    return pl.pallas_call(
        body,
        out_shape=(
            jax.ShapeDtypeStruct((rows // 2, width), F32),
            jax.ShapeDtypeStruct((rows // 2, 2 * width + half), BF),
        ),
        grid=(tiles,),
        in_specs=[rows_in] * len(flat)
        + [pl.BlockSpec((3, width, half), lambda t: (0, 0, 0))]
        + [pl.BlockSpec((tile, width), lambda t: (jnp.minimum(t, middle - 1), 0))]
        + [anywhere()] * len(deps),
        out_specs=[
            pl.BlockSpec((tile, width), lambda t: (jnp.maximum(t - middle, 0), 0)),
            pl.BlockSpec((tile, 2 * width + half), lambda t: (jnp.minimum(t, middle - 1), 0)),
        ],
        compiler_params=params(VMEM),
        cost_estimate=cost(6 * rows * width * half, 8e6),
    )(*flat, w_all, branch, *deps)


class Grid:
    def __init__(self):
        self.depth = lax.axis_size(NARROW)
        self.wide = lax.axis_size(WIDE)
        self.plane = self.wide // 2
        self.bits = self.plane.bit_length() - 1
        place = lax.axis_index(WIDE)
        self.core = place % 2
        self.chip = place // 2
        self.level = lax.axis_index(NARROW)

    def flip(self, label):
        return sum(((label >> b) & 1) << (self.bits - 1 - b) for b in range(self.bits))

    def chip_of(self, label):
        return self.chip ^ jnp.where(self.core == 0, label, self.flip(label))

    def label_of(self, chip):
        return jnp.where(self.core == 0, self.chip ^ chip, self.flip(self.chip ^ chip))

    def other(self, array):
        return lax.ppermute(array, WIDE, [(i, i ^ 1) for i in range(self.wide)])

    def hop(self, array, bit):
        pairs = []
        for i in range(self.wide):
            step = bit if i % 2 == 0 else self.bits - 1 - bit
            pairs.append((i, i ^ (2 << step)))
        return lax.ppermute(array, WIDE, pairs)

    def lift(self, array, distance):
        return lax.ppermute(array, NARROW, [(i, i ^ distance) for i in range(self.depth)])

    def lifts(self, block, first=None, wait=None):
        out = [block]
        for d in range(1, self.depth):
            low = d & -d
            if d <= 2 and first is not None:
                out.append(first[d - 1])
                continue
            source = out[d ^ low]
            if wait is not None and d != low:
                source = tie(source, wait)
            out.append(self.lift(source, low))
        return out

    def spots(self):
        return jnp.stack(
            [
                (self.level ^ d) * self.plane + self.chip_of(label)
                for label in range(self.plane)
                for d in range(self.depth)
            ]
        ).astype(jnp.int32)

    def spread(self, levels, first=None, wait=None):
        parts = [levels]
        for label in range(1, self.plane):
            top = label.bit_length() - 1
            source = parts[label ^ (1 << top)]
            if first is not None and label in (1, 1 << (self.bits - 1)):
                parts.append(first[0] if label == 1 else first[1])
                continue
            if wait is not None and source is not levels:
                source = tie(source, wait)
            parts.append(self.hop(source, top))
        return parts

    def fold(self, low, high, waits=(), ends=()):
        steps = [self.fold_step(low, high, self.bits - 1, waits[:1], ends[:1])]
        return steps + self.fold_rest(steps[0], waits[1:], ends[1:])

    def fold_rest(self, halves, waits=(), ends=()):
        steps = []
        for bit in range(self.bits - 2, -1, -1):
            n = len(steps)
            halves = self.fold_step(*halves, bit, waits[n : n + 1], ends[n : n + 1])
            steps.append(halves)
        return steps

    def fold_step(self, low, high, bit, waits=(), ends=()):
        for wait in waits:
            high = high if wait is None else tie(high, wait)
        came = self.hop(high, bit)
        for end in ends:
            low = low if end is None else tie(low, end)

        def added(a, b):
            return (a.astype(F32) + b.astype(F32)).astype(BF)

        if low.shape[0] == 1:
            return added(low[0], came[0])
        middle = low.shape[0] // 2
        return added(low[:middle], came[:middle]), added(low[middle:], came[middle:])

    def drop_all(self, blocks, ends=()):
        ends = list(ends)
        steps = []
        bit = 1
        while bit < self.depth:
            pairs = blocks.reshape((-1, 2) + blocks.shape[1:])
            came = self.lift(pairs[:, 1], bit).astype(F32)
            own = pairs[:, 0]
            if ends:
                own = tie(own, *ends.pop(0))
            total = own.astype(F32) + came
            bit *= 2
            blocks = total.astype(BF) if bit < self.depth else total
            steps.append(blocks)
        return steps[:-1] + [blocks[0]]


def tie(array, *deps):
    return lax.optimization_barrier((array,) + deps)[0]


def on_device(
    layer_in,
    first_values,
    out_grad,
    seq_group,
    short_split,
    attn_gain,
    mlp_gain,
    w_query,
    w_key,
    w_value,
    w_out,
    w_gate,
    w_up,
    w_down,
):
    grid = Grid()
    core = grid.core
    rows, width = layer_in.shape
    half = width // 2
    heads = half // HEAD_DIM
    shard = w_query.shape[0]
    block = 2 * shard

    def pick(first, second):
        return jnp.where(core == 0, first, second)

    split_own = jnp.where(seq_group[0] == 0, rows, short_split[0])
    gain_col = attn_gain.astype(F32)[:, None]
    w4 = [(gain_col * w.astype(F32)).astype(BF) for w in (w_query, w_key, w_value)] + [w_out.T]
    spare = jnp.zeros((16, half), BF).at[0, :shard].set(mlp_gain)
    spare = spare.at[1, :2].set(jnp.stack([split_own // 256, split_own % 256]).astype(BF))
    mine = jnp.concatenate([pick(w[:, :half], w[:, half:]) for w in w4] + [spare])
    came = grid.other(
        jnp.concatenate([pick(w[:, half:], w[:, :half]) for w in w4] + [spare])
    )
    split_other = came[4 * shard + 1, :2].astype(jnp.int32)
    split_other = split_other[0] * 256 + split_other[1]
    own_block = assemble(core.reshape(1).astype(jnp.int32), mine, came, shard)

    ff3 = jnp.stack([w_gate.T, w_up.T, w_down])
    units = ff3.shape[1] // 2
    cols = ff3.shape[2]
    ff_mine = pick(ff3[:, :units], ff3[:, units:])
    ff_came = grid.other(pick(ff3[:, units:], ff3[:, :units]))
    ff_block = pick(
        jnp.concatenate([ff_mine, ff_came], 2), jnp.concatenate([ff_came, ff_mine], 2)
    )

    fv_left, fv_right = first_values[:, :half], first_values[:, half:]
    sent = jnp.concatenate([layer_in, pick(fv_right, fv_left)], 1)
    got = grid.other(sent)
    x_other = got[:, :width]
    x2 = jnp.concatenate([layer_in, x_other]).astype(F32)
    fv2 = jnp.concatenate([pick(fv_left, fv_right), got[:, width:]])

    own_block = tie(own_block, got, ff_came)
    near_one = grid.hop(own_block, 0), grid.hop(own_block, grid.bits - 1)
    levels = grid.lifts(own_block)
    ff_own_block = tie(ff_block, *near_one)
    ff_own_one = grid.hop(ff_own_block, 0), grid.hop(ff_own_block, grid.bits - 1)
    level_blocks = tie(jnp.stack(levels[1:]), *near_one, *ff_own_one)
    ff_block_later = tie(ff_block, level_blocks)
    ff_first = grid.lift(ff_block_later, 1)
    far = grid.spread(level_blocks, wait=ff_first)
    near = grid.spread(own_block, first=near_one, wait=far[1])
    ff_own = grid.spread(ff_own_block, first=ff_own_one, wait=far[-1])
    ff_second = grid.lift(ff_block_later, 2)
    chips = jnp.stack([grid.chip_of(m) for m in range(grid.plane)]).astype(jnp.int32)
    spots = grid.spots()

    row_index = jnp.arange(rows, dtype=jnp.int32)
    splits = jnp.stack([split_own, split_other])
    lane = jnp.arange(128) % HEAD_DIM
    frequency = jnp.exp(
        (lane % (HEAD_DIM // 2)).astype(F32) * (-2.0 * math.log(10000.0) / HEAD_DIM)
    )
    second = row_index[None, :] >= splits[:, None]
    position = jnp.where(second, row_index[None, :] - splits[:, None], row_index[None, :])
    turned = position.astype(F32).reshape(-1)[:, None] * frequency[None, :]
    cos = jnp.cos(turned)
    sin = jnp.sin(turned) * jnp.where(lane < HEAD_DIM // 2, -1.0, 1.0)

    inv1 = rms_scale(x2)
    xhat = (x2 * inv1).astype(BF)
    queries, keys, values, w_all, out_mine, gains = project_rows(
        xhat, fv2, cos, sin, near, far, spots, block
    )
    out_other = grid.other(out_mine)
    og_other = grid.other(tie(out_grad, queries))
    ff_one = grid.spread(tie(ff_first, far[-1]), wait=queries)
    ff_third = grid.lift(tie(ff_second, queries), 1)
    ff_second_tied = tie(ff_second, queries)
    ff_two_one = grid.hop(ff_second_tied, 0), grid.hop(ff_second_tied, grid.bits - 1)
    attended, weights = attend(
        splits, queries, keys, values, deps=[ff_own[3], ff_one[1], ff_one[2], ff_second]
    )
    ff_two = grid.spread(ff_second_tied, first=ff_two_one, wait=attended)
    ff_three = grid.spread(tie(ff_third, attended))
    att_other = grid.other(tie(attended, ff_third))

    gain_mlp = gains.reshape(-1, 16, half)[:, :2, :shard].reshape(1, width).astype(F32)
    hidden, normed_two = out_and_norm(
        layer_in, x_other, attended, att_other, out_mine, out_other, gain_mlp
    )

    def feed(parts, before=None, deps=()):
        if parts[0][0].shape[-1] % 128 == 0:
            return feed_forward(chips, normed_two, out_grad, og_other, parts, before, deps)
        wholes = []
        for level in parts:
            stacked = jnp.stack(level)
            order = [stacked[grid.label_of(b)] for b in range(grid.plane)]
            wholes.append([jnp.concatenate(order, axis=-1)])
        sums, grads = feed_forward(
            chips, normed_two, out_grad, og_other, wholes, before, deps
        )
        grads = grads[0][0].reshape((3, -1, grid.plane, 2 * cols))
        grads = [grads[..., grid.chip_of(m), :] for m in range(grid.plane)]
        middle = grid.plane // 2
        return sums, [jnp.stack(grads[:middle]), jnp.stack(grads[middle:])]

    sums_a, grads_a = feed([ff_own], deps=[ff_two[2], ff_one[3]])
    sums_b, grads_b = feed([ff_one], before=sums_a, deps=[ff_three[1], ff_three[2], ff_two[3]])
    fold_a = grid.fold(*grads_a, waits=[None, sums_b[2]], ends=[sums_b[2]])
    sums, grads_c = feed([ff_two, ff_three], before=sums_b, deps=[fold_a[0][1]])
    branch, branch_sent, grad_nt = sums
    fold_b = [grid.fold_step(*grads_b, grid.bits - 1, ends=[grad_nt])]
    grad_nt_other = grid.other(tie(grad_nt, fold_a[-1], fold_b[0][1]))

    grad_hidden, grad_att, out_low, out_high = norm_two_back(
        spots, grad_nt, grad_nt_other, hidden, out_grad, og_other, gain_mlp,
        attended, out_mine, block, grid.plane,
    )
    pairs = half // 256
    fold_b += grid.fold_rest(fold_b[0], waits=[grad_nt], ends=[grad_att])
    lifted = grid.lift(fold_b[-1], 1)
    back_one = attend_back(
        queries, keys, values, weights, grad_att, cos, sin, 0, pairs, deps=[fold_b[-1]]
    )
    out_fold = grid.fold(out_low, out_high, waits=[None, back_one[0]], ends=[back_one[0]])
    fold_c = grid.fold(*grads_c, waits=[None, back_one[0]], ends=[grad_att])
    first = projection_grads(
        spots, xhat, back_one[:3], block, grid.plane, deps=[fold_c[0][1]]
    )
    back_two = attend_back(
        queries, keys, values, weights, grad_att, cos, sin, 1, pairs,
        deps=[lifted, out_fold[0][1], first[0]],
    )
    second = projection_grads(
        spots, xhat, back_two[:3], block, grid.plane, deps=[fold_c[-1]]
    )
    rest = [fold_c[-1][:, i * units : (i + 1) * units] for i in range(grid.depth - 2)]
    lifted_far = grid.lift(rest[1], 1)
    scaled_own, scaled_sent = rows_grad(
        (back_one[:3], back_two[:3]), w_all, branch_sent, deps=[second[0]]
    )
    second_fold = grid.fold(*second, ends=[scaled_own])
    first_fold = grid.fold(*first, waits=[None, second[0]], ends=[second[0], second_fold[0][1]])
    got = grid.other(scaled_sent)
    layer_out = hidden[:rows] + branch.astype(F32) + got[:, width : 2 * width].astype(F32)
    layer_out = layer_out.astype(BF)
    scaled_one = scaled_own + got[:, :width].astype(F32)
    v_keep = jnp.concatenate([back_one[3], back_two[3]], 1)
    v_got = got[:, 2 * width :].astype(F32)
    values_grad = pick(
        jnp.concatenate([v_keep, v_got], 1), jnp.concatenate([v_got, v_keep], 1)
    )
    x1 = layer_in.astype(F32)
    i1 = rms_scale(x1)
    in_grad = (
        grad_hidden
        + i1 * scaled_one
        - x1 * (i1 * i1 * i1) * jnp.mean(scaled_one * x1, axis=-1, keepdims=True)
    )
    second_levels = grid.drop_all(
        second_fold[-1], ends=[(scaled_own,), (in_grad, layer_out, values_grad)]
    )
    first_levels = grid.drop_all(first_fold[-1], ends=[(second_fold[-1],), (second_levels[-1],)])
    qkv_total = jnp.concatenate([first_levels[-1], second_levels[-1]], -1)
    qkv_total = qkv_total.reshape(3, block, half)
    out_total = grid.drop_all(out_fold[-1], ends=[(second_fold[0][1],), (second_levels[-1],)])[-1]

    kept = tie(fold_a[-1], second_levels[-1]).astype(F32) + lifted.astype(F32)
    passed = (tie(rest[0], second_fold[0][1]).astype(F32) + lifted_far.astype(F32)).astype(BF)
    total = kept + grid.lift(passed, 2).astype(F32)
    keep = pick(total[:, :, :cols], total[:, :, cols:])
    sent = pick(total[:, :, cols:], total[:, :, :cols]).astype(BF)
    got = grid.other(sent).astype(F32)
    ff_grads = pick(jnp.concatenate([keep, got], 1), jnp.concatenate([got, keep], 1))
    def own_rows(total):
        keep = pick(total[..., :shard, :], total[..., shard:, :])
        got = grid.other(pick(total[..., shard:, :], total[..., :shard, :]).astype(BF))
        got = got.astype(F32)
        return pick(jnp.concatenate([keep, got], -1), jnp.concatenate([got, keep], -1))

    plain = own_rows(qkv_total)
    attn_gain_grad = sum(
        jnp.sum(plain[k] * w.astype(F32), axis=-1)
        for k, w in enumerate((w_query, w_key, w_value))
    )
    out_proj_grad = own_rows(out_total[:block]).T
    gain_total = out_total[block]
    mlp_gain_grad = pick(gain_total[:shard], gain_total[shard : 2 * shard])
    return (
        layer_out,
        in_grad,
        values_grad,
        attn_gain_grad,
        mlp_gain_grad,
        gain_col * plain[0],
        gain_col * plain[1],
        gain_col * plain[2],
        out_proj_grad,
        ff_grads[0].T,
        ff_grads[1].T,
        ff_grads[2],
    )


def solution(mesh):
    rows = P((NARROW, WIDE), None)
    line = P((NARROW, WIDE))
    lanes = P(None, (NARROW, WIDE))
    return jax.shard_map(
        on_device,
        mesh=mesh,
        in_specs=(
            (rows,) * 3 + (line,) * 4 + (rows,) * 3
            + (lanes, P(WIDE, NARROW), P(WIDE, NARROW), P(NARROW, WIDE))
        ),
        out_specs=(
            (rows,) * 3 + (line,) * 2 + (rows,) * 3
            + (lanes, P(WIDE, NARROW), P(WIDE, NARROW), P(NARROW, WIDE))
        ),
        check_vma=False,
    )
```

```python
import math

import jax
import jax.numpy as jnp
from jax import lax
from jax.experimental import pallas as pl
from jax.experimental.pallas import tpu as pltpu
from jax.sharding import PartitionSpec as P

HEAD_DIM = 64
EPS = 1e-06
BF = jnp.bfloat16
F32 = jnp.float32
NARROW, WIDE = "narrow", "wide"
VMEM = 60
HEADS_AT_ONCE = 4


def dot(left, right, dims):
    return lax.dot_general(left, right, (dims, ((), ())), preferred_element_type=F32)


def nn(left, right):
    return dot(left, right, ((1,), (0,)))


def nt(left, right):
    return dot(left, right, ((1,), (1,)))


def tn(left, right):
    return dot(left, right, ((0,), (0,)))


def rms_scale(values):
    return lax.rsqrt(jnp.mean(values * values, axis=-1, keepdims=True) + EPS)


def tile_of(rows):
    return min(256, rows)


def anywhere():
    return pl.BlockSpec(memory_space=pl.ANY)


def in_smem():
    return pl.BlockSpec(memory_space=pltpu.SMEM)


def in_vmem():
    return pl.BlockSpec(memory_space=pltpu.VMEM)


def params(mib):
    return pltpu.CompilerParams(vmem_limit_bytes=mib * 1024 * 1024)


def cost(flops, moved):
    return pl.CostEstimate(
        flops=int(2 * flops), bytes_accessed=int(moved), transcendentals=0
    )


def turn(v, cos, sin):
    lane = lax.broadcasted_iota(jnp.int32, v.shape, 1)
    swapped = jnp.where(
        lane % HEAD_DIM < HEAD_DIM // 2,
        pltpu.roll(v, 128 - HEAD_DIM // 2, 1),
        pltpu.roll(v, HEAD_DIM // 2, 1),
    )
    return v * cos + swapped * sin


def assemble(core, mine, came, shard):
    half = mine.shape[1]

    def body(core_ref, mine_ref, came_ref, out_ref):
        own, other = mine_ref[...].astype(F32), came_ref[...].astype(F32)
        first = core_ref[0] == 0
        lower, upper = jnp.where(first, own, other), jnp.where(first, other, own)
        for k in range(4):
            at = slice(k * shard, (k + 1) * shard)
            pair = jnp.concatenate([lower[at], upper[at]], 0)
            out_ref[2 * k * shard : 2 * (k + 1) * shard] = pair.astype(BF)
        row = lax.broadcasted_iota(jnp.int32, (16, half), 0)
        spare = jnp.where(row == 0, lower[4 * shard : 4 * shard + 1], upper[4 * shard : 4 * shard + 1])
        out_ref[8 * shard :] = spare.astype(BF)

    return pl.pallas_call(
        body,
        out_shape=jax.ShapeDtypeStruct((8 * shard + 16, half), BF),
        in_specs=[in_smem(), in_vmem(), in_vmem()],
        out_specs=in_vmem(),
        compiler_params=params(VMEM),
    )(core, mine, came)


def project_rows(xhat, fv2, cos, sin, near, far, spots, block, deps=()):
    count, depth = len(near), far[0].shape[0] + 1
    blocks = count * depth
    rows, width = xhat.shape
    half = fv2.shape[1]
    tile = min(512, rows)

    def body(spot_ref, x_hbm, fv_hbm, cos_hbm, sin_hbm, *refs):
        refs = list(refs)
        sources = refs[: 2 * count]
        refs = refs[2 * count + len(deps) :]
        outs, w_out, wo_out, g_out = refs[:3], refs[3], refs[4], refs[5]
        x_ref, fv_ref, cos_ref, sin_ref, w_ref, wo_ref, g_ref, y_ref, sem, isem, osem = refs[6:]

        def weights(k):
            copies = []
            for m in range(count):
                for d in range(depth):
                    i = m * depth + d
                    source = sources[m] if d == 0 else sources[count + m].at[d - 1]
                    size = block if k < 4 else 16
                    to = pl.ds(pl.multiple_of(spot_ref[i] * size, size), size)
                    out = w_ref.at[k, to] if k < 3 else (wo_ref if k == 3 else g_ref).at[to]
                    copies.append(
                        pltpu.make_async_copy(source.at[pl.ds(k * block, size)], out, sem.at[k, i])
                    )
                    copies[-1].start()
            return copies

        ins = [
            pltpu.make_async_copy(a, b, isem.at[n])
            for n, (a, b) in enumerate(
                ((x_hbm, x_ref), (cos_hbm, cos_ref), (sin_hbm, sin_ref), (fv_hbm, fv_ref))
            )
        ]
        ins[0].start()
        arriving = [weights(0)]
        for c in ins[1:]:
            c.start()
        arriving += [weights(k) for k in range(1, 5)]
        for c in ins[:3]:
            c.wait()
        sends = []

        def send(source, to, n):
            sends.append(pltpu.make_async_copy(source, to, osem.at[n]))
            sends[-1].start()

        for k in range(3):
            for c in arriving[k]:
                c.wait()
            send(w_ref.at[k], w_out.at[k], k)
            if k == 2:
                ins[3].wait()
            for t in range(rows // tile):
                at = slice(t * tile, (t + 1) * tile)
                y = nn(x_ref[at], w_ref[k])
                if k == 2:
                    y_ref[k, at] = (0.5 * y + 0.5 * fv_ref[at].astype(F32)).astype(BF)
                else:
                    factor = HEAD_DIM ** (-0.5) if k == 0 else 1.0
                    cos_t, sin_t = cos_ref[at] * factor, sin_ref[at] * factor
                    for g in range(half // 128):
                        lanes = slice(g * 128, g * 128 + 128)
                        y_ref[k, at, lanes] = turn(y[:, lanes], cos_t, sin_t).astype(BF)
            send(y_ref.at[k], outs[k], 3 + k)
        for k, (source, to) in ((3, (wo_ref, wo_out)), (4, (g_ref, g_out))):
            for c in arriving[k]:
                c.wait()
            send(source, to, 3 + k)
        for c in sends:
            c.wait()

    shape = jax.ShapeDtypeStruct((rows, half), BF)
    return pl.pallas_call(
        body,
        out_shape=(
            shape,
            shape,
            shape,
            jax.ShapeDtypeStruct((3, width, half), BF),
            jax.ShapeDtypeStruct((width, half), BF),
            jax.ShapeDtypeStruct((16 * blocks, half), BF),
        ),
        in_specs=[in_smem()] + [anywhere()] * (4 + 2 * count + len(deps)),
        out_specs=[anywhere()] * 6,
        scratch_shapes=[
            pltpu.VMEM((rows, width), BF),
            pltpu.VMEM((rows, half), BF),
            pltpu.VMEM((rows, 128), F32),
            pltpu.VMEM((rows, 128), F32),
            pltpu.VMEM((3, width, half), BF),
            pltpu.VMEM((width, half), BF),
            pltpu.VMEM((16 * blocks, half), BF),
            pltpu.VMEM((3, rows, half), BF),
            pltpu.SemaphoreType.DMA((5, blocks)),
            pltpu.SemaphoreType.DMA((4,)),
            pltpu.SemaphoreType.DMA((8,)),
        ],
        compiler_params=params(VMEM),
        cost_estimate=cost(6 * rows * width * half, 12e6),
    )(spots, xhat, fv2, cos, sin, *near, *far, *deps)


def query_blocks(rows):
    step = tile_of(rows)
    return [(s, step, s + step) for s in range(0, rows, step)]


def attend(splits, queries, keys, values, deps=()):
    rows2, half = queries.shape
    rows = rows2 // 2
    group = min(HEADS_AT_ONCE, half // HEAD_DIM)
    lanes = group * HEAD_DIM
    groups = half // lanes

    def body(split_ref, q_ref, k_ref, v_ref, *refs):
        o_ref, p_ref, bias, v_t = refs[len(deps) :]
        slot = pl.program_id(0)

        @pl.when(pl.program_id(1) == 0)
        def _():
            split = split_ref[slot]
            key = lax.broadcasted_iota(jnp.int32, (rows, rows), 0)
            query = lax.broadcasted_iota(jnp.int32, (rows, rows), 1)
            low = jnp.where(query >= split, split, 0)
            bias[...] = jnp.where((key <= query) & (key >= low), 0.0, -1e30)

        v_t[...] = v_ref[...].T
        lane = lax.broadcasted_iota(jnp.int32, (rows, 128), 1)
        feature = lax.broadcasted_iota(jnp.int32, (128, 1), 0)
        chains = [
            (block, h) for block in reversed(query_blocks(rows)) for h in range(group)
        ]

        def scores(chain):
            (start, count, key_end), h = chain
            at = slice(start, start + count)
            pair = slice(h // 2 * 128, h // 2 * 128 + 128)
            in_head = (lane[:key_end] < 64) if h % 2 == 0 else (lane[:key_end] >= 64)
            k = jnp.where(in_head, k_ref[:key_end, pair], 0)
            return nt(k, q_ref[at, pair]) + bias[:key_end, at]

        ahead = scores(chains[0])
        outs = []
        for i, chain in enumerate(chains):
            (start, count, key_end), h = chain
            at = slice(start, start + count)
            pair = slice(h // 2 * 128, h // 2 * 128 + 128)
            s = ahead
            if i + 1 < len(chains):
                ahead = scores(chains[i + 1])
            e = jnp.exp(s - jnp.max(s, axis=0, keepdims=True))
            p = (e * (1.0 / jnp.sum(e, axis=0, keepdims=True))).astype(BF)
            p_ref[h, :key_end, at] = p
            outs.append(nn(v_t[pair, :key_end], p))
            if h % 2 == 1:
                o = jnp.where(feature < 64, outs[-2], outs[-1])
                o_ref[at, pair] = o.astype(BF).T

    spec = pl.BlockSpec((rows, lanes), lambda s, p, *_: (s, p))
    return pl.pallas_call(
        body,
        out_shape=(
            jax.ShapeDtypeStruct((rows2, half), BF),
            jax.ShapeDtypeStruct((2 * half // HEAD_DIM, rows, rows), BF),
        ),
        grid_spec=pltpu.PrefetchScalarGridSpec(
            num_scalar_prefetch=1,
            grid=(2, groups),
            in_specs=[spec] * 3 + [anywhere()] * len(deps),
            out_specs=[
                spec,
                pl.BlockSpec((group, rows, rows), lambda s, p, *_: (s * groups + p, 0, 0)),
            ],
            scratch_shapes=[pltpu.VMEM((rows, rows), F32), pltpu.VMEM((lanes, rows), BF)],
        ),
        compiler_params=params(VMEM),
        cost_estimate=cost(16 * rows * rows * half, 12e6),
    )(splits, queries, keys, values, *deps)


def attend_back(queries, keys, values, weights, grad_att, cos, sin, start, pairs, deps=()):
    rows2, half = queries.shape
    rows = rows2 // 2
    lanes = 128 * pairs
    group = 2 * pairs
    groups = half // lanes
    blocks = query_blocks(rows)

    def body(q_ref, k_ref, v_ref, p_ref, ga_ref, cos_ref, sin_ref, *refs):
        gq_ref, gk_ref, gv_ref, own_ref, k_t, gs_sc = refs[len(deps) :]
        k_t[...] = k_ref[...].T
        lane = lax.broadcasted_iota(jnp.int32, (rows, 128), 1)
        feature = lax.broadcasted_iota(jnp.int32, (128, 1), 0)
        chains = [(h, block) for h in range(group) for block in blocks]

        def pair_of(h):
            return slice(h // 2 * 128, h // 2 * 128 + 128)

        def grad_probs(chain):
            h, (first, count, key_end) = chain
            in_head = (lane[:key_end] < 64) if h % 2 == 0 else (lane[:key_end] >= 64)
            v = jnp.where(in_head, v_ref[:key_end, pair_of(h)], 0)
            return nt(v, ga_ref[first : first + count, pair_of(h)])

        ahead = grad_probs(chains[0])
        gq, gk, gv = {}, {}, {}
        for i, (h, (first, count, key_end)) in enumerate(chains):
            at, pair = slice(first, first + count), pair_of(h)
            gp = ahead
            if i + 1 < len(chains):
                ahead = grad_probs(chains[i + 1])
            pf = p_ref[h, :key_end, at].astype(F32)
            delta = jnp.sum(gp * pf, axis=0, keepdims=True)
            gs = (pf * (gp - delta)).astype(BF)
            gs_sc[h % 2, :key_end, at] = gs
            gq[h, first] = nn(k_t[pair, :key_end], gs)
            if first + count < rows:
                continue
            for low, size, _ in blocks:
                mine = slice(low, low + size)
                gk[h, low] = nn(gs_sc[h % 2, mine, low:], q_ref[low:, pair])
                gv[h, low] = nn(p_ref[h, mine, low:], ga_ref[low:, pair])
            if h % 2 == 0:
                continue
            for low, size, _ in blocks:
                mine = slice(low, low + size)
                c, s = cos_ref[mine], -sin_ref[mine]
                both = jnp.where(feature < 64, gq[h - 1, low], gq[h, low])
                gq_ref[mine, pair] = turn((both * HEAD_DIM ** (-0.5)).T, c, s).astype(BF)
                both = jnp.where(lane[:size] < 64, gk[h - 1, low], gk[h, low])
                gk_ref[mine, pair] = turn(both, c, s).astype(BF)
                both = 0.5 * jnp.where(lane[:size] < 64, gv[h - 1, low], gv[h, low])
                gv_ref[mine, pair] = both.astype(BF)

                @pl.when(pl.program_id(0) == 0)
                def _():
                    own_ref[mine, pair] = both

    spec = pl.BlockSpec((rows, lanes), lambda s: (s, start))
    out = pl.BlockSpec((rows, lanes), lambda s: (s, 0))
    table = pl.BlockSpec((rows, 128), lambda s: (s, 0))
    shape = jax.ShapeDtypeStruct((rows2, lanes), BF)
    return pl.pallas_call(
        body,
        out_shape=(shape, shape, shape, jax.ShapeDtypeStruct((rows, lanes), F32)),
        grid=(2,),
        in_specs=[spec] * 3
        + [pl.BlockSpec((group, rows, rows), lambda s: (s * groups + start, 0, 0))]
        + [spec, table, table]
        + [anywhere()] * len(deps),
        out_specs=[out] * 3 + [pl.BlockSpec((rows, lanes), lambda s: (0, 0))],
        scratch_shapes=[pltpu.VMEM((lanes, rows), BF), pltpu.VMEM((2, rows, rows), BF)],
        compiler_params=params(VMEM),
        cost_estimate=cost(32 * rows * rows * lanes, 8e6),
    )(queries, keys, values, weights, grad_att, cos, sin, *deps)


def feed_forward(chips, normed_two, og_own, og_other, parts, before=None, deps=()):
    levels, count = len(parts), len(parts[0])
    _, each, lanes = parts[0][0].shape
    units = levels * each
    flat = [a for level in parts for a in level]
    rows, width = normed_two.shape
    tile = min(512, rows // 2)
    tiles = rows // tile
    more = 0 if before is None else 3
    groups = min(2, count)
    low = count // groups

    def body(chip_ref, nt_hbm, og_first, og_second, *refs):
        ins, refs = refs[: len(flat)], refs[len(flat) :]
        olds = refs[:more]
        refs = refs[more + len(deps) :]
        br_outs, gn_hbm, outs = refs[:2], refs[2], refs[3 : 3 + groups]
        x_all, o_all, w, act, gg, gu, ob, br, gn, rsem, wsem, osem, psem = refs[3 + groups :]

        def lanes_at(m):
            if count == 1:
                return slice(None)
            return pl.ds(pl.multiple_of(chip_ref[m] * lanes, lanes), lanes)

        def rows_at(t):
            return pl.ds(t * tile, tile)

        row_in, weight_in, old_in = [], [], []
        per_core = tiles // 2

        def part_of(pair, t):
            return pair[t // per_core].at[rows_at(t % per_core)]

        for t in range(tiles):
            row_in.append((
                pltpu.make_async_copy(nt_hbm.at[rows_at(t)], x_all.at[rows_at(t)], rsem.at[0, t]),
                pltpu.make_async_copy(
                    part_of((og_first, og_second), t), o_all.at[rows_at(t)], rsem.at[1, t]
                ),
            ))
            old_in.append([])
            if more:
                old_in[t].append(
                    pltpu.make_async_copy(part_of(olds[:2], t), br.at[rows_at(t)], psem.at[0, t])
                )
                old_in[t].append(
                    pltpu.make_async_copy(olds[2].at[rows_at(t)], gn.at[rows_at(t)], psem.at[1, t])
                )
        for k in range(3):
            weight_in.append([
                pltpu.make_async_copy(
                    ins[v * count + m].at[k],
                    w.at[k, pl.ds(v * each, each), lanes_at(m)],
                    wsem.at[k, v * count + m],
                )
                for v in range(levels)
                for m in range(count)
            ])
        row_in[0][0].start()
        for k in range(3):
            for c in weight_in[k]:
                c.start()
            if k == 1:
                row_in[0][1].start()
        for t in range(1, tiles):
            row_in[t][0].start()
            row_in[t][1].start()
        for t in range(tiles):
            for c in old_in[t]:
                c.start()

        sends = []
        for t in range(tiles):
            at = rows_at(t)
            row_in[t][0].wait()
            x = x_all[at]
            if t == 0:
                for c in weight_in[0]:
                    c.wait()
            gate = nt(w[0], x)
            if t == 0:
                for c in weight_in[1]:
                    c.wait()
            up = nt(w[1], x)
            row_in[t][1].wait()
            if t == 0:
                for c in weight_in[2]:
                    c.wait()
            ga = nt(w[2], o_all[at])
            sig = jax.nn.sigmoid(gate)
            soft = gate * sig
            a = (soft * up).astype(BF)
            g = (ga * up * (sig + soft * (1.0 - sig))).astype(BF)
            u = (ga * soft).astype(BF)
            act[:, at] = a
            gg[:, at] = g
            gu[:, at] = u
            b = tn(a, w[2])
            n = tn(g, w[0]) + tn(u, w[1])
            if more:
                for c in old_in[t]:
                    c.wait()
                b = b + br[at].astype(F32)
                n = n + gn[at].astype(F32)
            br[at] = b.astype(BF)
            gn[at] = n.astype(BF)
            sends.append(pltpu.make_async_copy(br.at[at], part_of(br_outs, t), rsem.at[0, t]))
            sends.append(pltpu.make_async_copy(gn.at[at], gn_hbm.at[at], rsem.at[1, t]))
            sends[-2].start()
            sends[-1].start()

        for m in reversed(range(count)):
            at = lanes_at(m)
            x, o = x_all[:, at], o_all[:, at]
            for k, left, right in ((0, gg, x), (1, gu, x), (2, act, o)):
                ob[m, k] = nn(left[...], right).astype(BF)
            sends.append(pltpu.make_async_copy(ob.at[m], outs[m // low].at[m % low], osem.at[m]))
            sends[-1].start()
        for c in sends:
            c.wait()

    shape = jax.ShapeDtypeStruct((rows, width), BF)
    part_rows = jax.ShapeDtypeStruct((rows // 2, width), BF)
    part = jax.ShapeDtypeStruct((low, 3, units, lanes), BF)
    out = pl.pallas_call(
        body,
        out_shape=(part_rows, part_rows, shape) + (part,) * groups,
        in_specs=[in_smem()] + [anywhere()] * (3 + len(flat) + more + len(deps)),
        out_specs=[anywhere()] * (3 + groups),
        scratch_shapes=[
            pltpu.VMEM((rows, width), BF),
            pltpu.VMEM((rows, width), BF),
            pltpu.VMEM((3, units, width), BF),
            pltpu.VMEM((units, rows), BF),
            pltpu.VMEM((units, rows), BF),
            pltpu.VMEM((units, rows), BF),
            pltpu.VMEM((count, 3, units, lanes), BF),
            pltpu.VMEM((rows, width), BF),
            pltpu.VMEM((rows, width), BF),
            pltpu.SemaphoreType.DMA((2, tiles)),
            pltpu.SemaphoreType.DMA((3, len(flat))),
            pltpu.SemaphoreType.DMA((count,)),
            pltpu.SemaphoreType.DMA((2, tiles)),
        ],
        compiler_params=params(VMEM),
        cost_estimate=cost(18 * rows * width * units, 12e6),
    )(chips, normed_two, og_own, og_other, *flat, *(before or ()), *deps)
    return out[:3], list(out[3:])


def out_and_norm(x_own, x_other, attended, att_other, out_mine, out_other, gain, deps=()):
    rows, half = attended.shape
    width = x_own.shape[1]
    tile = tile_of(rows // 2)
    tiles = rows // tile
    middle = tiles // 2

    def body(xa_ref, xb_ref, a_ref, b_ref, wa_ref, wb_ref, gain_ref, *refs):
        h_ref, n_ref = refs[len(deps) :]
        x = jnp.where(pl.program_id(0) < middle, xa_ref[...], xb_ref[...])
        h = x.astype(F32) + nt(a_ref[...], wa_ref[...]) + nt(b_ref[...], wb_ref[...])
        h_ref[...] = h
        n_ref[...] = (h * rms_scale(h) * gain_ref[...]).astype(BF)

    def rows_of(width, shift=0):
        return pl.BlockSpec((tile, width), lambda t: ((t + shift) % tiles, 0))

    def whole(a):
        return pl.BlockSpec(a.shape, lambda t: (0, 0))

    return pl.pallas_call(
        body,
        out_shape=(
            jax.ShapeDtypeStruct((rows, width), F32),
            jax.ShapeDtypeStruct((rows, width), BF),
        ),
        grid=(tiles,),
        in_specs=[
            pl.BlockSpec((tile, width), lambda t: (jnp.minimum(t, middle - 1), 0)),
            pl.BlockSpec((tile, width), lambda t: (jnp.maximum(t - middle, 0), 0)),
            rows_of(half),
            rows_of(half, middle),
            whole(out_mine),
            whole(out_other),
            whole(gain),
        ]
        + [anywhere()] * len(deps),
        out_specs=[rows_of(width)] * 2,
        compiler_params=params(VMEM),
        cost_estimate=cost(4 * rows * width * half, 12e6),
    )(x_own, x_other, attended, att_other, out_mine, out_other, gain, *deps)


def norm_two_back(spots, grad_nt, grad_nt_other, hidden, og_own, og_other, gain, attended, out_mine, block, labels, deps=()):
    rows, width = hidden.shape
    half = attended.shape[1]
    tile = tile_of(rows // 2)
    tiles = rows // tile
    middle = tiles // 2
    blocks = width // block
    depth = blocks // labels
    low = labels // 2
    size = block + 16

    def body(spot_ref, g_ref, r_ref, h_ref, oa_ref, ob_ref, gain_ref, a_ref, w_ref, *refs):
        gh_ref, ga_ref, lo_ref, hi_ref, acc, gains, all_blocks, sem = refs[len(deps) :]
        t = pl.program_id(0)
        h = h_ref[...]
        g = g_ref[...].astype(F32) + r_ref[...].astype(F32)
        dz = jnp.where(t < middle, oa_ref[...], ob_ref[...]).astype(F32)
        inv = rms_scale(h)
        scaled = g * gain_ref[...]
        grad = dz + inv * scaled - h * (
            inv * inv * inv * jnp.mean(scaled * h, axis=-1, keepdims=True)
        )

        @pl.when(t < middle)
        def _():
            gh_ref[...] = grad

        branch = grad.astype(BF)
        ga_ref[...] = nn(branch, w_ref[...]).astype(BF)
        part = tn(branch, a_ref[...])
        gain_part = jnp.sum(g * h * inv, axis=0, keepdims=True)

        @pl.when(t == 0)
        def _():
            acc[...] = part
            gains[...] = gain_part

        @pl.when(t > 0)
        def _():
            acc[...] += part
            gains[...] += gain_part

        @pl.when(t == tiles - 1)
        def _():
            all_blocks[:, block:] = jnp.zeros((blocks, 16, half), BF)
            for i in range(blocks):
                all_blocks[i, :block] = acc[i * block : (i + 1) * block].astype(BF)
                all_blocks[i, block : block + 1, :block] = gains[
                    :, i * block : (i + 1) * block
                ].astype(BF)
            copies = []
            for m in range(labels):
                out = lo_ref if m < low else hi_ref
                for d in range(depth):
                    i = m * depth + d
                    copies.append(
                        pltpu.make_async_copy(
                            all_blocks.at[spot_ref[i]], out.at[m % low, d], sem.at[i]
                        )
                    )
            for c in copies:
                c.start()
            for c in copies:
                c.wait()

    def rows_of(width, shift=0):
        return pl.BlockSpec((tile, width), lambda t: ((t + shift) % tiles, 0))

    def whole(a):
        return pl.BlockSpec(a.shape, lambda t: (0, 0))

    part = jax.ShapeDtypeStruct((low, depth, size, half), BF)
    first = pl.BlockSpec((tile, width), lambda t: (jnp.minimum(t, middle - 1), 0))
    second = pl.BlockSpec((tile, width), lambda t: (jnp.maximum(t - middle, 0), 0))
    return pl.pallas_call(
        body,
        out_shape=(
            jax.ShapeDtypeStruct((rows // 2, width), F32),
            jax.ShapeDtypeStruct((rows, half), BF),
            part,
            part,
        ),
        grid=(tiles,),
        in_specs=[
            in_smem(),
            rows_of(width),
            rows_of(width, middle),
            rows_of(width),
            first,
            second,
            whole(gain),
            rows_of(half),
            whole(out_mine),
        ]
        + [anywhere()] * len(deps),
        out_specs=[first, rows_of(half), anywhere(), anywhere()],
        scratch_shapes=[
            pltpu.VMEM((width, half), F32),
            pltpu.VMEM((1, width), F32),
            pltpu.VMEM((blocks, size, half), BF),
            pltpu.SemaphoreType.DMA((blocks,)),
        ],
        compiler_params=params(VMEM),
        cost_estimate=cost(4 * rows * width * half, 20e6),
    )(spots, grad_nt, grad_nt_other, hidden, og_own, og_other, gain, attended, out_mine, *deps)


def projection_grads(spots, xhat, grads, block, labels, deps=()):
    rows, width = xhat.shape
    count = len(grads)
    half = grads[0].shape[1]
    blocks = width // block
    depth = blocks // labels
    low = labels // 2

    def body(spot_ref, x_ref, *refs):
        ins = refs[:count]
        lo_ref, hi_ref, out, sem = refs[count + len(deps) :]
        x_t = x_ref[...].T
        copies = []
        for k in range(count):
            out[k] = nn(x_t, ins[k][...]).astype(BF)
            for m in range(labels):
                to = lo_ref if m < low else hi_ref
                for d in range(depth):
                    i = m * depth + d
                    start = pl.multiple_of(spot_ref[i] * block, block)
                    copies.append(
                        pltpu.make_async_copy(
                            out.at[k, pl.ds(start, block)],
                            to.at[m % low, d, pl.ds(k * block, block)],
                            sem.at[k, i],
                        )
                    )
                    copies[-1].start()
        for c in copies:
            c.wait()

    part = jax.ShapeDtypeStruct((low, depth, count * block, half), BF)
    return pl.pallas_call(
        body,
        out_shape=(part, part),
        in_specs=[in_smem()] + [in_vmem()] * (1 + count) + [anywhere()] * len(deps),
        out_specs=[anywhere()] * 2,
        scratch_shapes=[
            pltpu.VMEM((count, width, half), BF),
            pltpu.SemaphoreType.DMA((count, blocks)),
        ],
        compiler_params=params(VMEM),
        cost_estimate=cost(2 * count * rows * width * half, 8e6),
    )(spots, xhat, *grads, *deps)


def rows_grad(grads, w_all, branch, deps=()):
    rows, lanes = grads[0][0].shape
    width, half = w_all.shape[1:]
    flat = [g for group in grads for g in group]
    tile = tile_of(rows // 2)
    tiles = rows // tile
    middle = tiles // 2

    def body(*refs):
        ins, w_ref, b_ref = refs[: len(flat)], refs[len(flat)], refs[len(flat) + 1]
        own_ref, other_ref = refs[len(flat) + 2 + len(deps) :]
        t = pl.program_id(0)
        y = None
        for k in range(3):
            g = jnp.concatenate([ins[3 * i + k][...] for i in range(len(grads))], 1)
            part = nt(g, w_ref[k])
            y = part if y is None else y + part

        @pl.when(t < middle)
        def _():
            other_ref[:, :width] = y.astype(BF)
            other_ref[:, width : 2 * width] = b_ref[...]
            for i in range(len(grads)):
                other_ref[:, 2 * width + i * lanes : 2 * width + (i + 1) * lanes] = ins[3 * i + 2][...]

        @pl.when(t >= middle)
        def _():
            own_ref[...] = y

    rows_in = pl.BlockSpec((tile, lanes), lambda t: ((t + middle) % tiles, 0))
    return pl.pallas_call(
        body,
        out_shape=(
            jax.ShapeDtypeStruct((rows // 2, width), F32),
            jax.ShapeDtypeStruct((rows // 2, 2 * width + half), BF),
        ),
        grid=(tiles,),
        in_specs=[rows_in] * len(flat)
        + [pl.BlockSpec((3, width, half), lambda t: (0, 0, 0))]
        + [pl.BlockSpec((tile, width), lambda t: (jnp.minimum(t, middle - 1), 0))]
        + [anywhere()] * len(deps),
        out_specs=[
            pl.BlockSpec((tile, width), lambda t: (jnp.maximum(t - middle, 0), 0)),
            pl.BlockSpec((tile, 2 * width + half), lambda t: (jnp.minimum(t, middle - 1), 0)),
        ],
        compiler_params=params(VMEM),
        cost_estimate=cost(6 * rows * width * half, 8e6),
    )(*flat, w_all, branch, *deps)


class Grid:
    def __init__(self):
        self.depth = lax.axis_size(NARROW)
        self.wide = lax.axis_size(WIDE)
        self.plane = self.wide // 2
        self.bits = self.plane.bit_length() - 1
        place = lax.axis_index(WIDE)
        self.core = place % 2
        self.chip = place // 2
        self.level = lax.axis_index(NARROW)

    def flip(self, label):
        return sum(((label >> b) & 1) << (self.bits - 1 - b) for b in range(self.bits))

    def chip_of(self, label):
        return self.chip ^ jnp.where(self.core == 0, label, self.flip(label))

    def label_of(self, chip):
        return jnp.where(self.core == 0, self.chip ^ chip, self.flip(self.chip ^ chip))

    def other(self, array):
        return lax.ppermute(array, WIDE, [(i, i ^ 1) for i in range(self.wide)])

    def hop(self, array, bit):
        pairs = []
        for i in range(self.wide):
            step = bit if i % 2 == 0 else self.bits - 1 - bit
            pairs.append((i, i ^ (2 << step)))
        return lax.ppermute(array, WIDE, pairs)

    def lift(self, array, distance):
        return lax.ppermute(array, NARROW, [(i, i ^ distance) for i in range(self.depth)])

    def lifts(self, block, first=None, wait=None):
        out = [block]
        for d in range(1, self.depth):
            low = d & -d
            if d <= 2 and first is not None:
                out.append(first[d - 1])
                continue
            source = out[d ^ low]
            if wait is not None and d != low:
                source = tie(source, wait)
            out.append(self.lift(source, low))
        return out

    def spots(self):
        return jnp.stack(
            [
                (self.level ^ d) * self.plane + self.chip_of(label)
                for label in range(self.plane)
                for d in range(self.depth)
            ]
        ).astype(jnp.int32)

    def spread(self, levels, first=None, wait=None):
        parts = [levels]
        for label in range(1, self.plane):
            top = label.bit_length() - 1
            source = parts[label ^ (1 << top)]
            if first is not None and label in (1, 1 << (self.bits - 1)):
                parts.append(first[0] if label == 1 else first[1])
                continue
            if wait is not None and source is not levels:
                source = tie(source, wait)
            parts.append(self.hop(source, top))
        return parts

    def fold(self, low, high, waits=(), ends=()):
        steps = [self.fold_step(low, high, self.bits - 1, waits[:1], ends[:1])]
        return steps + self.fold_rest(steps[0], waits[1:], ends[1:])

    def fold_rest(self, halves, waits=(), ends=()):
        steps = []
        for bit in range(self.bits - 2, -1, -1):
            n = len(steps)
            halves = self.fold_step(*halves, bit, waits[n : n + 1], ends[n : n + 1])
            steps.append(halves)
        return steps

    def fold_step(self, low, high, bit, waits=(), ends=()):
        for wait in waits:
            high = high if wait is None else tie(high, wait)
        came = self.hop(high, bit)
        for end in ends:
            low = low if end is None else tie(low, end)

        def added(a, b):
            return (a.astype(F32) + b.astype(F32)).astype(BF)

        if low.shape[0] == 1:
            return added(low[0], came[0])
        middle = low.shape[0] // 2
        return added(low[:middle], came[:middle]), added(low[middle:], came[middle:])

    def drop_all(self, blocks, ends=()):
        ends = list(ends)
        steps = []
        bit = 1
        while bit < self.depth:
            pairs = blocks.reshape((-1, 2) + blocks.shape[1:])
            came = self.lift(pairs[:, 1], bit).astype(F32)
            own = pairs[:, 0]
            if ends:
                own = tie(own, *ends.pop(0))
            total = own.astype(F32) + came
            bit *= 2
            blocks = total.astype(BF) if bit < self.depth else total
            steps.append(blocks)
        return steps[:-1] + [blocks[0]]


def tie(array, *deps):
    return lax.optimization_barrier((array,) + deps)[0]


def on_device(
    layer_in,
    first_values,
    out_grad,
    seq_group,
    short_split,
    attn_gain,
    mlp_gain,
    w_query,
    w_key,
    w_value,
    w_out,
    w_gate,
    w_up,
    w_down,
):
    grid = Grid()
    core = grid.core
    rows, width = layer_in.shape
    half = width // 2
    heads = half // HEAD_DIM
    shard = w_query.shape[0]
    block = 2 * shard

    def pick(first, second):
        return jnp.where(core == 0, first, second)

    split_own = jnp.where(seq_group[0] == 0, rows, short_split[0])
    gain_col = attn_gain.astype(F32)[:, None]
    w4 = [(gain_col * w.astype(F32)).astype(BF) for w in (w_query, w_key, w_value)] + [w_out.T]
    spare = jnp.zeros((16, half), BF).at[0, :shard].set(mlp_gain)
    spare = spare.at[1, :2].set(jnp.stack([split_own // 256, split_own % 256]).astype(BF))
    mine = jnp.concatenate([pick(w[:, :half], w[:, half:]) for w in w4] + [spare])
    came = grid.other(
        jnp.concatenate([pick(w[:, half:], w[:, :half]) for w in w4] + [spare])
    )
    split_other = came[4 * shard + 1, :2].astype(jnp.int32)
    split_other = split_other[0] * 256 + split_other[1]
    own_block = assemble(core.reshape(1).astype(jnp.int32), mine, came, shard)

    ff3 = jnp.stack([w_gate.T, w_up.T, w_down])
    units = ff3.shape[1] // 2
    cols = ff3.shape[2]
    ff_mine = pick(ff3[:, :units], ff3[:, units:])
    ff_came = grid.other(pick(ff3[:, units:], ff3[:, :units]))
    ff_block = pick(
        jnp.concatenate([ff_mine, ff_came], 2), jnp.concatenate([ff_came, ff_mine], 2)
    )

    fv_left, fv_right = first_values[:, :half], first_values[:, half:]
    sent = jnp.concatenate([layer_in, pick(fv_right, fv_left)], 1)
    got = grid.other(sent)
    x_other = got[:, :width]
    x2 = jnp.concatenate([layer_in, x_other]).astype(F32)
    fv2 = jnp.concatenate([pick(fv_left, fv_right), got[:, width:]])

    own_block = tie(own_block, got, ff_came)
    near_one = grid.hop(own_block, 0), grid.hop(own_block, grid.bits - 1)
    levels = grid.lifts(own_block)
    ff_own_block = tie(ff_block, *near_one)
    ff_own_one = grid.hop(ff_own_block, 0), grid.hop(ff_own_block, grid.bits - 1)
    level_blocks = tie(jnp.stack(levels[1:]), *near_one, *ff_own_one)
    ff_block_later = tie(ff_block, level_blocks)
    ff_first = grid.lift(ff_block_later, 1)
    far = grid.spread(level_blocks, wait=ff_first)
    near = grid.spread(own_block, first=near_one, wait=far[1])
    ff_own = grid.spread(ff_own_block, first=ff_own_one, wait=far[-1])
    ff_second = grid.lift(ff_block_later, 2)
    chips = jnp.stack([grid.chip_of(m) for m in range(grid.plane)]).astype(jnp.int32)
    spots = grid.spots()

    row_index = jnp.arange(rows, dtype=jnp.int32)
    splits = jnp.stack([split_own, split_other])
    lane = jnp.arange(128) % HEAD_DIM
    frequency = jnp.exp(
        (lane % (HEAD_DIM // 2)).astype(F32) * (-2.0 * math.log(10000.0) / HEAD_DIM)
    )
    second = row_index[None, :] >= splits[:, None]
    position = jnp.where(second, row_index[None, :] - splits[:, None], row_index[None, :])
    turned = position.astype(F32).reshape(-1)[:, None] * frequency[None, :]
    cos = jnp.cos(turned)
    sin = jnp.sin(turned) * jnp.where(lane < HEAD_DIM // 2, -1.0, 1.0)

    inv1 = rms_scale(x2)
    xhat = (x2 * inv1).astype(BF)
    queries, keys, values, w_all, out_mine, gains = project_rows(
        xhat, fv2, cos, sin, near, far, spots, block
    )
    out_other = grid.other(out_mine)
    og_other = grid.other(tie(out_grad, queries))
    ff_one = grid.spread(tie(ff_first, far[-1]), wait=queries)
    ff_third = grid.lift(tie(ff_second, queries), 1)
    ff_second_tied = tie(ff_second, queries)
    ff_two_one = grid.hop(ff_second_tied, 0), grid.hop(ff_second_tied, grid.bits - 1)
    attended, weights = attend(
        splits, queries, keys, values, deps=[ff_own[3], ff_one[1], ff_one[2], ff_second]
    )
    ff_two = grid.spread(ff_second_tied, first=ff_two_one, wait=attended)
    ff_three = grid.spread(tie(ff_third, attended))
    att_other = grid.other(tie(attended, ff_third))

    gain_mlp = gains.reshape(-1, 16, half)[:, :2, :shard].reshape(1, width).astype(F32)
    hidden, normed_two = out_and_norm(
        layer_in, x_other, attended, att_other, out_mine, out_other, gain_mlp
    )

    def feed(parts, before=None, deps=()):
        if parts[0][0].shape[-1] % 128 == 0:
            return feed_forward(chips, normed_two, out_grad, og_other, parts, before, deps)
        wholes = []
        for level in parts:
            stacked = jnp.stack(level)
            order = [stacked[grid.label_of(b)] for b in range(grid.plane)]
            wholes.append([jnp.concatenate(order, axis=-1)])
        sums, grads = feed_forward(
            chips, normed_two, out_grad, og_other, wholes, before, deps
        )
        grads = grads[0][0].reshape((3, -1, grid.plane, 2 * cols))
        grads = [grads[..., grid.chip_of(m), :] for m in range(grid.plane)]
        middle = grid.plane // 2
        return sums, [jnp.stack(grads[:middle]), jnp.stack(grads[middle:])]

    sums_a, grads_a = feed([ff_own], deps=[ff_two[2]])
    sums_b, grads_b = feed([ff_one], before=sums_a, deps=[ff_three[1], ff_three[2], ff_two[3]])
    fold_a = grid.fold(*grads_a, waits=[None, sums_b[2]], ends=[sums_b[2]])
    sums, grads_c = feed([ff_two, ff_three], before=sums_b, deps=[fold_a[0][1]])
    branch, branch_sent, grad_nt = sums
    fold_b = [grid.fold_step(*grads_b, grid.bits - 1, ends=[grad_nt])]
    grad_nt_other = grid.other(tie(grad_nt, fold_a[-1], fold_b[0][1]))

    grad_hidden, grad_att, out_low, out_high = norm_two_back(
        spots, grad_nt, grad_nt_other, hidden, out_grad, og_other, gain_mlp,
        attended, out_mine, block, grid.plane,
    )
    pairs = half // 256
    fold_b += grid.fold_rest(fold_b[0], waits=[grad_nt], ends=[grad_att])
    lifted = grid.lift(fold_b[-1], 1)
    back_one = attend_back(
        queries, keys, values, weights, grad_att, cos, sin, 0, pairs, deps=[fold_b[-1]]
    )
    out_fold = [grid.fold_step(out_low, out_high, grid.bits - 1, ends=[back_one[0]])]
    fold_c = grid.fold(*grads_c, waits=[None, back_one[0]], ends=[grad_att])
    first = projection_grads(
        spots, xhat, back_one[:3], block, grid.plane, deps=[fold_c[0][1]]
    )
    back_two = attend_back(
        queries, keys, values, weights, grad_att, cos, sin, 1, pairs,
        deps=[lifted, out_fold[0][1], first[0]],
    )
    second = projection_grads(
        spots, xhat, back_two[:3], block, grid.plane, deps=[fold_c[-1]]
    )
    rest = [fold_c[-1][:, i * units : (i + 1) * units] for i in range(grid.depth - 2)]
    lifted_far = grid.lift(rest[1], 1)
    scaled_own, scaled_sent = rows_grad(
        (back_one[:3], back_two[:3]), w_all, branch_sent, deps=[second[0]]
    )
    second_fold = grid.fold(*second, ends=[scaled_own])
    out_fold += grid.fold_rest(out_fold[0], waits=[back_one[0]], ends=[second[0]])
    first_fold = grid.fold(*first, waits=[None, second[0]], ends=[second[0], second_fold[0][1]])
    got = grid.other(scaled_sent)
    layer_out = hidden[:rows] + branch.astype(F32) + got[:, width : 2 * width].astype(F32)
    layer_out = layer_out.astype(BF)
    scaled_one = scaled_own + got[:, :width].astype(F32)
    v_keep = jnp.concatenate([back_one[3], back_two[3]], 1)
    v_got = got[:, 2 * width :].astype(F32)
    values_grad = pick(
        jnp.concatenate([v_keep, v_got], 1), jnp.concatenate([v_got, v_keep], 1)
    )
    x1 = layer_in.astype(F32)
    i1 = rms_scale(x1)
    in_grad = (
        grad_hidden
        + i1 * scaled_one
        - x1 * (i1 * i1 * i1) * jnp.mean(scaled_one * x1, axis=-1, keepdims=True)
    )
    second_levels = grid.drop_all(
        second_fold[-1], ends=[(scaled_own,), (in_grad, layer_out, values_grad)]
    )
    first_levels = grid.drop_all(first_fold[-1], ends=[(second_fold[-1],), (second_levels[-1],)])
    qkv_total = jnp.concatenate([first_levels[-1], second_levels[-1]], -1)
    qkv_total = qkv_total.reshape(3, block, half)
    out_total = grid.drop_all(out_fold[-1], ends=[(second_fold[0][1],), (second_levels[-1],)])[-1]

    kept = tie(fold_a[-1], second_levels[-1]).astype(F32) + lifted.astype(F32)
    passed = (tie(rest[0], second_fold[0][1]).astype(F32) + lifted_far.astype(F32)).astype(BF)
    total = kept + grid.lift(passed, 2).astype(F32)
    keep = pick(total[:, :, :cols], total[:, :, cols:])
    sent = pick(total[:, :, cols:], total[:, :, :cols]).astype(BF)
    got = grid.other(sent).astype(F32)
    ff_grads = pick(jnp.concatenate([keep, got], 1), jnp.concatenate([got, keep], 1))
    def own_rows(total):
        keep = pick(total[..., :shard, :], total[..., shard:, :])
        got = grid.other(pick(total[..., shard:, :], total[..., :shard, :]).astype(BF))
        got = got.astype(F32)
        return pick(jnp.concatenate([keep, got], -1), jnp.concatenate([got, keep], -1))

    plain = own_rows(qkv_total)
    attn_gain_grad = sum(
        jnp.sum(plain[k] * w.astype(F32), axis=-1)
        for k, w in enumerate((w_query, w_key, w_value))
    )
    out_proj_grad = own_rows(out_total[:block]).T
    gain_total = out_total[block]
    mlp_gain_grad = pick(gain_total[:shard], gain_total[shard : 2 * shard])
    return (
        layer_out,
        in_grad,
        values_grad,
        attn_gain_grad,
        mlp_gain_grad,
        gain_col * plain[0],
        gain_col * plain[1],
        gain_col * plain[2],
        out_proj_grad,
        ff_grads[0].T,
        ff_grads[1].T,
        ff_grads[2],
    )


def solution(mesh):
    rows = P((NARROW, WIDE), None)
    line = P((NARROW, WIDE))
    lanes = P(None, (NARROW, WIDE))
    return jax.shard_map(
        on_device,
        mesh=mesh,
        in_specs=(
            (rows,) * 3 + (line,) * 4 + (rows,) * 3
            + (lanes, P(WIDE, NARROW), P(WIDE, NARROW), P(NARROW, WIDE))
        ),
        out_specs=(
            (rows,) * 3 + (line,) * 2 + (rows,) * 3
            + (lanes, P(WIDE, NARROW), P(WIDE, NARROW), P(NARROW, WIDE))
        ),
        check_vma=False,
    )
```

```python
import math

import jax
import jax.numpy as jnp
from jax import lax
from jax.experimental import pallas as pl
from jax.experimental.pallas import tpu as pltpu
from jax.sharding import PartitionSpec as P

HEAD_DIM = 64
EPS = 1e-06
BF = jnp.bfloat16
F32 = jnp.float32
NARROW, WIDE = "narrow", "wide"
VMEM = 60
HEADS_AT_ONCE = 4


def dot(left, right, dims):
    return lax.dot_general(left, right, (dims, ((), ())), preferred_element_type=F32)


def nn(left, right):
    return dot(left, right, ((1,), (0,)))


def nt(left, right):
    return dot(left, right, ((1,), (1,)))


def tn(left, right):
    return dot(left, right, ((0,), (0,)))


def rms_scale(values):
    return lax.rsqrt(jnp.mean(values * values, axis=-1, keepdims=True) + EPS)


def tile_of(rows):
    return min(256, rows)


def anywhere():
    return pl.BlockSpec(memory_space=pl.ANY)


def in_smem():
    return pl.BlockSpec(memory_space=pltpu.SMEM)


def in_vmem():
    return pl.BlockSpec(memory_space=pltpu.VMEM)


def params(mib):
    return pltpu.CompilerParams(vmem_limit_bytes=mib * 1024 * 1024)


def cost(flops, moved):
    return pl.CostEstimate(
        flops=int(2 * flops), bytes_accessed=int(moved), transcendentals=0
    )


def turn(v, cos, sin):
    lane = lax.broadcasted_iota(jnp.int32, v.shape, 1)
    swapped = jnp.where(
        lane % HEAD_DIM < HEAD_DIM // 2,
        pltpu.roll(v, 128 - HEAD_DIM // 2, 1),
        pltpu.roll(v, HEAD_DIM // 2, 1),
    )
    return v * cos + swapped * sin


def assemble(core, mine, came, shard):
    half = mine.shape[1]

    def body(core_ref, mine_ref, came_ref, out_ref):
        own, other = mine_ref[...].astype(F32), came_ref[...].astype(F32)
        first = core_ref[0] == 0
        lower, upper = jnp.where(first, own, other), jnp.where(first, other, own)
        for k in range(4):
            at = slice(k * shard, (k + 1) * shard)
            pair = jnp.concatenate([lower[at], upper[at]], 0)
            out_ref[2 * k * shard : 2 * (k + 1) * shard] = pair.astype(BF)
        row = lax.broadcasted_iota(jnp.int32, (16, half), 0)
        spare = jnp.where(row == 0, lower[4 * shard : 4 * shard + 1], upper[4 * shard : 4 * shard + 1])
        out_ref[8 * shard :] = spare.astype(BF)

    return pl.pallas_call(
        body,
        out_shape=jax.ShapeDtypeStruct((8 * shard + 16, half), BF),
        in_specs=[in_smem(), in_vmem(), in_vmem()],
        out_specs=in_vmem(),
        compiler_params=params(VMEM),
    )(core, mine, came)


def project_rows(xhat, fv2, cos, sin, near, far, spots, block, deps=()):
    count, depth = len(near), far[0].shape[0] + 1
    blocks = count * depth
    rows, width = xhat.shape
    half = fv2.shape[1]
    tile = min(512, rows)

    def body(spot_ref, x_hbm, fv_hbm, cos_hbm, sin_hbm, *refs):
        refs = list(refs)
        sources = refs[: 2 * count]
        refs = refs[2 * count + len(deps) :]
        outs, w_out, wo_out, g_out = refs[:3], refs[3], refs[4], refs[5]
        x_ref, fv_ref, cos_ref, sin_ref, w_ref, wo_ref, g_ref, y_ref, sem, isem, osem = refs[6:]

        def weights(k):
            copies = []
            for m in range(count):
                for d in range(depth):
                    i = m * depth + d
                    source = sources[m] if d == 0 else sources[count + m].at[d - 1]
                    size = block if k < 4 else 16
                    to = pl.ds(pl.multiple_of(spot_ref[i] * size, size), size)
                    out = w_ref.at[k, to] if k < 3 else (wo_ref if k == 3 else g_ref).at[to]
                    copies.append(
                        pltpu.make_async_copy(source.at[pl.ds(k * block, size)], out, sem.at[k, i])
                    )
                    copies[-1].start()
            return copies

        ins = [
            pltpu.make_async_copy(a, b, isem.at[n])
            for n, (a, b) in enumerate(
                ((x_hbm, x_ref), (cos_hbm, cos_ref), (sin_hbm, sin_ref), (fv_hbm, fv_ref))
            )
        ]
        ins[0].start()
        arriving = [weights(0)]
        for c in ins[1:]:
            c.start()
        arriving += [weights(k) for k in range(1, 5)]
        for c in ins[:3]:
            c.wait()
        sends = []

        def send(source, to, n):
            sends.append(pltpu.make_async_copy(source, to, osem.at[n]))
            sends[-1].start()

        for k in range(3):
            for c in arriving[k]:
                c.wait()
            send(w_ref.at[k], w_out.at[k], k)
            if k == 2:
                ins[3].wait()
            for t in range(rows // tile):
                at = slice(t * tile, (t + 1) * tile)
                y = nn(x_ref[at], w_ref[k])
                if k == 2:
                    y_ref[k, at] = (0.5 * y + 0.5 * fv_ref[at].astype(F32)).astype(BF)
                else:
                    factor = HEAD_DIM ** (-0.5) if k == 0 else 1.0
                    cos_t, sin_t = cos_ref[at] * factor, sin_ref[at] * factor
                    for g in range(half // 128):
                        lanes = slice(g * 128, g * 128 + 128)
                        y_ref[k, at, lanes] = turn(y[:, lanes], cos_t, sin_t).astype(BF)
            send(y_ref.at[k], outs[k], 3 + k)
        for k, (source, to) in ((3, (wo_ref, wo_out)), (4, (g_ref, g_out))):
            for c in arriving[k]:
                c.wait()
            send(source, to, 3 + k)
        for c in sends:
            c.wait()

    shape = jax.ShapeDtypeStruct((rows, half), BF)
    return pl.pallas_call(
        body,
        out_shape=(
            shape,
            shape,
            shape,
            jax.ShapeDtypeStruct((3, width, half), BF),
            jax.ShapeDtypeStruct((width, half), BF),
            jax.ShapeDtypeStruct((16 * blocks, half), BF),
        ),
        in_specs=[in_smem()] + [anywhere()] * (4 + 2 * count + len(deps)),
        out_specs=[anywhere()] * 6,
        scratch_shapes=[
            pltpu.VMEM((rows, width), BF),
            pltpu.VMEM((rows, half), BF),
            pltpu.VMEM((rows, 128), F32),
            pltpu.VMEM((rows, 128), F32),
            pltpu.VMEM((3, width, half), BF),
            pltpu.VMEM((width, half), BF),
            pltpu.VMEM((16 * blocks, half), BF),
            pltpu.VMEM((3, rows, half), BF),
            pltpu.SemaphoreType.DMA((5, blocks)),
            pltpu.SemaphoreType.DMA((4,)),
            pltpu.SemaphoreType.DMA((8,)),
        ],
        compiler_params=params(VMEM),
        cost_estimate=cost(6 * rows * width * half, 12e6),
    )(spots, xhat, fv2, cos, sin, *near, *far, *deps)


def query_blocks(rows):
    step = tile_of(rows)
    return [(s, step, s + step) for s in range(0, rows, step)]


def attend(splits, queries, keys, values, deps=()):
    rows2, half = queries.shape
    rows = rows2 // 2
    group = min(HEADS_AT_ONCE, half // HEAD_DIM)
    lanes = group * HEAD_DIM
    groups = half // lanes

    def body(split_ref, q_ref, k_ref, v_ref, *refs):
        o_ref, p_ref, bias, v_t = refs[len(deps) :]
        slot = pl.program_id(0)

        @pl.when(pl.program_id(1) == 0)
        def _():
            split = split_ref[slot]
            key = lax.broadcasted_iota(jnp.int32, (rows, rows), 0)
            query = lax.broadcasted_iota(jnp.int32, (rows, rows), 1)
            low = jnp.where(query >= split, split, 0)
            bias[...] = jnp.where((key <= query) & (key >= low), 0.0, -1e30)

        v_t[...] = v_ref[...].T
        lane = lax.broadcasted_iota(jnp.int32, (rows, 128), 1)
        feature = lax.broadcasted_iota(jnp.int32, (128, 1), 0)
        chains = [
            (block, h) for block in reversed(query_blocks(rows)) for h in range(group)
        ]

        def scores(chain):
            (start, count, key_end), h = chain
            at = slice(start, start + count)
            pair = slice(h // 2 * 128, h // 2 * 128 + 128)
            in_head = (lane[:key_end] < 64) if h % 2 == 0 else (lane[:key_end] >= 64)
            k = jnp.where(in_head, k_ref[:key_end, pair], 0)
            return nt(k, q_ref[at, pair]) + bias[:key_end, at]

        ahead = scores(chains[0])
        outs = []
        for i, chain in enumerate(chains):
            (start, count, key_end), h = chain
            at = slice(start, start + count)
            pair = slice(h // 2 * 128, h // 2 * 128 + 128)
            s = ahead
            if i + 1 < len(chains):
                ahead = scores(chains[i + 1])
            e = jnp.exp(s - jnp.max(s, axis=0, keepdims=True))
            p = (e * (1.0 / jnp.sum(e, axis=0, keepdims=True))).astype(BF)
            p_ref[h, :key_end, at] = p
            outs.append(nn(v_t[pair, :key_end], p))
            if h % 2 == 1:
                o = jnp.where(feature < 64, outs[-2], outs[-1])
                o_ref[at, pair] = o.astype(BF).T

    spec = pl.BlockSpec((rows, lanes), lambda s, p, *_: (s, p))
    return pl.pallas_call(
        body,
        out_shape=(
            jax.ShapeDtypeStruct((rows2, half), BF),
            jax.ShapeDtypeStruct((2 * half // HEAD_DIM, rows, rows), BF),
        ),
        grid_spec=pltpu.PrefetchScalarGridSpec(
            num_scalar_prefetch=1,
            grid=(2, groups),
            in_specs=[spec] * 3 + [anywhere()] * len(deps),
            out_specs=[
                spec,
                pl.BlockSpec((group, rows, rows), lambda s, p, *_: (s * groups + p, 0, 0)),
            ],
            scratch_shapes=[pltpu.VMEM((rows, rows), F32), pltpu.VMEM((lanes, rows), BF)],
        ),
        compiler_params=params(VMEM),
        cost_estimate=cost(16 * rows * rows * half, 12e6),
    )(splits, queries, keys, values, *deps)


def attend_back(queries, keys, values, weights, grad_att, cos, sin, start, pairs, deps=()):
    rows2, half = queries.shape
    rows = rows2 // 2
    lanes = 128 * pairs
    group = 2 * pairs
    groups = half // lanes
    blocks = query_blocks(rows)

    def body(q_ref, k_ref, v_ref, p_ref, ga_ref, cos_ref, sin_ref, *refs):
        gq_ref, gk_ref, gv_ref, own_ref, k_t, gs_sc = refs[len(deps) :]
        k_t[...] = k_ref[...].T
        lane = lax.broadcasted_iota(jnp.int32, (rows, 128), 1)
        feature = lax.broadcasted_iota(jnp.int32, (128, 1), 0)
        chains = [(h, block) for h in range(group) for block in blocks]

        def pair_of(h):
            return slice(h // 2 * 128, h // 2 * 128 + 128)

        def grad_probs(chain):
            h, (first, count, key_end) = chain
            in_head = (lane[:key_end] < 64) if h % 2 == 0 else (lane[:key_end] >= 64)
            v = jnp.where(in_head, v_ref[:key_end, pair_of(h)], 0)
            return nt(v, ga_ref[first : first + count, pair_of(h)])

        ahead = grad_probs(chains[0])
        gq, gk, gv = {}, {}, {}
        for i, (h, (first, count, key_end)) in enumerate(chains):
            at, pair = slice(first, first + count), pair_of(h)
            gp = ahead
            if i + 1 < len(chains):
                ahead = grad_probs(chains[i + 1])
            pf = p_ref[h, :key_end, at].astype(F32)
            delta = jnp.sum(gp * pf, axis=0, keepdims=True)
            gs = (pf * (gp - delta)).astype(BF)
            gs_sc[h % 2, :key_end, at] = gs
            gq[h, first] = nn(k_t[pair, :key_end], gs)
            if first + count < rows:
                continue
            for low, size, _ in blocks:
                mine = slice(low, low + size)
                gk[h, low] = nn(gs_sc[h % 2, mine, low:], q_ref[low:, pair])
                gv[h, low] = nn(p_ref[h, mine, low:], ga_ref[low:, pair])
            if h % 2 == 0:
                continue
            for low, size, _ in blocks:
                mine = slice(low, low + size)
                c, s = cos_ref[mine], -sin_ref[mine]
                both = jnp.where(feature < 64, gq[h - 1, low], gq[h, low])
                gq_ref[mine, pair] = turn((both * HEAD_DIM ** (-0.5)).T, c, s).astype(BF)
                both = jnp.where(lane[:size] < 64, gk[h - 1, low], gk[h, low])
                gk_ref[mine, pair] = turn(both, c, s).astype(BF)
                both = 0.5 * jnp.where(lane[:size] < 64, gv[h - 1, low], gv[h, low])
                gv_ref[mine, pair] = both.astype(BF)

                @pl.when(pl.program_id(0) == 0)
                def _():
                    own_ref[mine, pair] = both

    spec = pl.BlockSpec((rows, lanes), lambda s: (s, start))
    out = pl.BlockSpec((rows, lanes), lambda s: (s, 0))
    table = pl.BlockSpec((rows, 128), lambda s: (s, 0))
    shape = jax.ShapeDtypeStruct((rows2, lanes), BF)
    return pl.pallas_call(
        body,
        out_shape=(shape, shape, shape, jax.ShapeDtypeStruct((rows, lanes), F32)),
        grid=(2,),
        in_specs=[spec] * 3
        + [pl.BlockSpec((group, rows, rows), lambda s: (s * groups + start, 0, 0))]
        + [spec, table, table]
        + [anywhere()] * len(deps),
        out_specs=[out] * 3 + [pl.BlockSpec((rows, lanes), lambda s: (0, 0))],
        scratch_shapes=[pltpu.VMEM((lanes, rows), BF), pltpu.VMEM((2, rows, rows), BF)],
        compiler_params=params(VMEM),
        cost_estimate=cost(32 * rows * rows * lanes, 8e6),
    )(queries, keys, values, weights, grad_att, cos, sin, *deps)


def feed_forward(chips, normed_two, og_own, og_other, parts, before=None, deps=()):
    levels, count = len(parts), len(parts[0])
    _, each, lanes = parts[0][0].shape
    units = levels * each
    flat = [a for level in parts for a in level]
    rows, width = normed_two.shape
    tile = min(512, rows // 2)
    tiles = rows // tile
    more = 0 if before is None else 3
    groups = min(2, count)
    low = count // groups

    def body(chip_ref, nt_hbm, og_first, og_second, *refs):
        ins, refs = refs[: len(flat)], refs[len(flat) :]
        olds = refs[:more]
        refs = refs[more + len(deps) :]
        br_outs, gn_hbm, outs = refs[:2], refs[2], refs[3 : 3 + groups]
        x_all, o_all, w, act, gg, gu, ob, br, gn, rsem, wsem, osem, psem = refs[3 + groups :]

        def lanes_at(m):
            if count == 1:
                return slice(None)
            return pl.ds(pl.multiple_of(chip_ref[m] * lanes, lanes), lanes)

        def rows_at(t):
            return pl.ds(t * tile, tile)

        row_in, weight_in, old_in = [], [], []
        per_core = tiles // 2

        def part_of(pair, t):
            return pair[t // per_core].at[rows_at(t % per_core)]

        for t in range(tiles):
            row_in.append((
                pltpu.make_async_copy(nt_hbm.at[rows_at(t)], x_all.at[rows_at(t)], rsem.at[0, t]),
                pltpu.make_async_copy(
                    part_of((og_first, og_second), t), o_all.at[rows_at(t)], rsem.at[1, t]
                ),
            ))
            old_in.append([])
            if more:
                old_in[t].append(
                    pltpu.make_async_copy(part_of(olds[:2], t), br.at[rows_at(t)], psem.at[0, t])
                )
                old_in[t].append(
                    pltpu.make_async_copy(olds[2].at[rows_at(t)], gn.at[rows_at(t)], psem.at[1, t])
                )
        for k in range(3):
            weight_in.append([
                pltpu.make_async_copy(
                    ins[v * count + m].at[k],
                    w.at[k, pl.ds(v * each, each), lanes_at(m)],
                    wsem.at[k, v * count + m],
                )
                for v in range(levels)
                for m in range(count)
            ])
        row_in[0][0].start()
        for k in range(3):
            for c in weight_in[k]:
                c.start()
            if k == 1:
                row_in[0][1].start()
        for t in range(1, tiles):
            row_in[t][0].start()
            row_in[t][1].start()
        for t in range(tiles):
            for c in old_in[t]:
                c.start()

        sends = []
        for t in range(tiles):
            at = rows_at(t)
            row_in[t][0].wait()
            x = x_all[at]
            if t == 0:
                for c in weight_in[0]:
                    c.wait()
            gate = nt(w[0], x)
            if t == 0:
                for c in weight_in[1]:
                    c.wait()
            up = nt(w[1], x)
            row_in[t][1].wait()
            if t == 0:
                for c in weight_in[2]:
                    c.wait()
            ga = nt(w[2], o_all[at])
            sig = jax.nn.sigmoid(gate)
            soft = gate * sig
            a = (soft * up).astype(BF)
            g = (ga * up * (sig + soft * (1.0 - sig))).astype(BF)
            u = (ga * soft).astype(BF)
            act[:, at] = a
            gg[:, at] = g
            gu[:, at] = u
            b = tn(a, w[2])
            n = tn(g, w[0]) + tn(u, w[1])
            if more:
                for c in old_in[t]:
                    c.wait()
                b = b + br[at].astype(F32)
                n = n + gn[at].astype(F32)
            br[at] = b.astype(BF)
            gn[at] = n.astype(BF)
            sends.append(pltpu.make_async_copy(br.at[at], part_of(br_outs, t), rsem.at[0, t]))
            sends.append(pltpu.make_async_copy(gn.at[at], gn_hbm.at[at], rsem.at[1, t]))
            sends[-2].start()
            sends[-1].start()

        for m in reversed(range(count)):
            at = lanes_at(m)
            x, o = x_all[:, at], o_all[:, at]
            for k, left, right in ((0, gg, x), (1, gu, x), (2, act, o)):
                ob[m, k] = nn(left[...], right).astype(BF)
            sends.append(pltpu.make_async_copy(ob.at[m], outs[m // low].at[m % low], osem.at[m]))
            sends[-1].start()
        for c in sends:
            c.wait()

    shape = jax.ShapeDtypeStruct((rows, width), BF)
    part_rows = jax.ShapeDtypeStruct((rows // 2, width), BF)
    part = jax.ShapeDtypeStruct((low, 3, units, lanes), BF)
    out = pl.pallas_call(
        body,
        out_shape=(part_rows, part_rows, shape) + (part,) * groups,
        in_specs=[in_smem()] + [anywhere()] * (3 + len(flat) + more + len(deps)),
        out_specs=[anywhere()] * (3 + groups),
        scratch_shapes=[
            pltpu.VMEM((rows, width), BF),
            pltpu.VMEM((rows, width), BF),
            pltpu.VMEM((3, units, width), BF),
            pltpu.VMEM((units, rows), BF),
            pltpu.VMEM((units, rows), BF),
            pltpu.VMEM((units, rows), BF),
            pltpu.VMEM((count, 3, units, lanes), BF),
            pltpu.VMEM((rows, width), BF),
            pltpu.VMEM((rows, width), BF),
            pltpu.SemaphoreType.DMA((2, tiles)),
            pltpu.SemaphoreType.DMA((3, len(flat))),
            pltpu.SemaphoreType.DMA((count,)),
            pltpu.SemaphoreType.DMA((2, tiles)),
        ],
        compiler_params=params(VMEM),
        cost_estimate=cost(18 * rows * width * units, 12e6),
    )(chips, normed_two, og_own, og_other, *flat, *(before or ()), *deps)
    return out[:3], list(out[3:])


def out_and_norm(x_own, x_other, attended, att_other, out_mine, out_other, gain, deps=()):
    rows, half = attended.shape
    width = x_own.shape[1]
    tile = tile_of(rows // 2)
    tiles = rows // tile
    middle = tiles // 2

    def body(xa_ref, xb_ref, a_ref, b_ref, wa_ref, wb_ref, gain_ref, *refs):
        h_ref, n_ref = refs[len(deps) :]
        x = jnp.where(pl.program_id(0) < middle, xa_ref[...], xb_ref[...])
        h = x.astype(F32) + nt(a_ref[...], wa_ref[...]) + nt(b_ref[...], wb_ref[...])
        h_ref[...] = h
        n_ref[...] = (h * rms_scale(h) * gain_ref[...]).astype(BF)

    def rows_of(width, shift=0):
        return pl.BlockSpec((tile, width), lambda t: ((t + shift) % tiles, 0))

    def whole(a):
        return pl.BlockSpec(a.shape, lambda t: (0, 0))

    return pl.pallas_call(
        body,
        out_shape=(
            jax.ShapeDtypeStruct((rows, width), F32),
            jax.ShapeDtypeStruct((rows, width), BF),
        ),
        grid=(tiles,),
        in_specs=[
            pl.BlockSpec((tile, width), lambda t: (jnp.minimum(t, middle - 1), 0)),
            pl.BlockSpec((tile, width), lambda t: (jnp.maximum(t - middle, 0), 0)),
            rows_of(half),
            rows_of(half, middle),
            whole(out_mine),
            whole(out_other),
            whole(gain),
        ]
        + [anywhere()] * len(deps),
        out_specs=[rows_of(width)] * 2,
        compiler_params=params(VMEM),
        cost_estimate=cost(4 * rows * width * half, 12e6),
    )(x_own, x_other, attended, att_other, out_mine, out_other, gain, *deps)


def norm_two_back(spots, grad_nt, grad_nt_other, hidden, og_own, og_other, gain, attended, out_mine, block, labels, deps=()):
    rows, width = hidden.shape
    half = attended.shape[1]
    tile = tile_of(rows // 2)
    tiles = rows // tile
    middle = tiles // 2
    blocks = width // block
    depth = blocks // labels
    low = labels // 2
    size = block + 16

    def body(spot_ref, g_ref, r_ref, h_ref, oa_ref, ob_ref, gain_ref, a_ref, w_ref, *refs):
        gh_ref, ga_ref, lo_ref, hi_ref, acc, gains, all_blocks, sem = refs[len(deps) :]
        t = pl.program_id(0)
        h = h_ref[...]
        g = g_ref[...].astype(F32) + r_ref[...].astype(F32)
        dz = jnp.where(t < middle, oa_ref[...], ob_ref[...]).astype(F32)
        inv = rms_scale(h)
        scaled = g * gain_ref[...]
        grad = dz + inv * scaled - h * (
            inv * inv * inv * jnp.mean(scaled * h, axis=-1, keepdims=True)
        )

        @pl.when(t < middle)
        def _():
            gh_ref[...] = grad

        branch = grad.astype(BF)
        ga_ref[...] = nn(branch, w_ref[...]).astype(BF)
        part = tn(branch, a_ref[...])
        gain_part = jnp.sum(g * h * inv, axis=0, keepdims=True)

        @pl.when(t == 0)
        def _():
            acc[...] = part
            gains[...] = gain_part

        @pl.when(t > 0)
        def _():
            acc[...] += part
            gains[...] += gain_part

        @pl.when(t == tiles - 1)
        def _():
            all_blocks[:, block:] = jnp.zeros((blocks, 16, half), BF)
            for i in range(blocks):
                all_blocks[i, :block] = acc[i * block : (i + 1) * block].astype(BF)
                all_blocks[i, block : block + 1, :block] = gains[
                    :, i * block : (i + 1) * block
                ].astype(BF)
            copies = []
            for m in range(labels):
                out = lo_ref if m < low else hi_ref
                for d in range(depth):
                    i = m * depth + d
                    copies.append(
                        pltpu.make_async_copy(
                            all_blocks.at[spot_ref[i]], out.at[m % low, d], sem.at[i]
                        )
                    )
            for c in copies:
                c.start()
            for c in copies:
                c.wait()

    def rows_of(width, shift=0):
        return pl.BlockSpec((tile, width), lambda t: ((t + shift) % tiles, 0))

    def whole(a):
        return pl.BlockSpec(a.shape, lambda t: (0, 0))

    part = jax.ShapeDtypeStruct((low, depth, size, half), BF)
    first = pl.BlockSpec((tile, width), lambda t: (jnp.minimum(t, middle - 1), 0))
    second = pl.BlockSpec((tile, width), lambda t: (jnp.maximum(t - middle, 0), 0))
    return pl.pallas_call(
        body,
        out_shape=(
            jax.ShapeDtypeStruct((rows // 2, width), F32),
            jax.ShapeDtypeStruct((rows, half), BF),
            part,
            part,
        ),
        grid=(tiles,),
        in_specs=[
            in_smem(),
            rows_of(width),
            rows_of(width, middle),
            rows_of(width),
            first,
            second,
            whole(gain),
            rows_of(half),
            whole(out_mine),
        ]
        + [anywhere()] * len(deps),
        out_specs=[first, rows_of(half), anywhere(), anywhere()],
        scratch_shapes=[
            pltpu.VMEM((width, half), F32),
            pltpu.VMEM((1, width), F32),
            pltpu.VMEM((blocks, size, half), BF),
            pltpu.SemaphoreType.DMA((blocks,)),
        ],
        compiler_params=params(VMEM),
        cost_estimate=cost(4 * rows * width * half, 20e6),
    )(spots, grad_nt, grad_nt_other, hidden, og_own, og_other, gain, attended, out_mine, *deps)


def projection_grads(spots, xhat, grads, block, labels, deps=()):
    rows, width = xhat.shape
    count = len(grads)
    half = grads[0].shape[1]
    blocks = width // block
    depth = blocks // labels
    low = labels // 2

    def body(spot_ref, x_ref, *refs):
        ins = refs[:count]
        lo_ref, hi_ref, out, sem = refs[count + len(deps) :]
        x_t = x_ref[...].T
        copies = []
        for k in range(count):
            out[k] = nn(x_t, ins[k][...]).astype(BF)
            for m in range(labels):
                to = lo_ref if m < low else hi_ref
                for d in range(depth):
                    i = m * depth + d
                    start = pl.multiple_of(spot_ref[i] * block, block)
                    copies.append(
                        pltpu.make_async_copy(
                            out.at[k, pl.ds(start, block)],
                            to.at[m % low, d, pl.ds(k * block, block)],
                            sem.at[k, i],
                        )
                    )
                    copies[-1].start()
        for c in copies:
            c.wait()

    part = jax.ShapeDtypeStruct((low, depth, count * block, half), BF)
    return pl.pallas_call(
        body,
        out_shape=(part, part),
        in_specs=[in_smem()] + [in_vmem()] * (1 + count) + [anywhere()] * len(deps),
        out_specs=[anywhere()] * 2,
        scratch_shapes=[
            pltpu.VMEM((count, width, half), BF),
            pltpu.SemaphoreType.DMA((count, blocks)),
        ],
        compiler_params=params(VMEM),
        cost_estimate=cost(2 * count * rows * width * half, 8e6),
    )(spots, xhat, *grads, *deps)


def rows_grad(grads, w_all, branch, deps=()):
    rows, lanes = grads[0][0].shape
    width, half = w_all.shape[1:]
    flat = [g for group in grads for g in group]
    tile = tile_of(rows // 2)
    tiles = rows // tile
    middle = tiles // 2

    def body(*refs):
        ins, w_ref, b_ref = refs[: len(flat)], refs[len(flat)], refs[len(flat) + 1]
        own_ref, other_ref = refs[len(flat) + 2 + len(deps) :]
        t = pl.program_id(0)
        y = None
        for k in range(3):
            g = jnp.concatenate([ins[3 * i + k][...] for i in range(len(grads))], 1)
            part = nt(g, w_ref[k])
            y = part if y is None else y + part

        @pl.when(t < middle)
        def _():
            other_ref[:, :width] = y.astype(BF)
            other_ref[:, width : 2 * width] = b_ref[...]
            for i in range(len(grads)):
                other_ref[:, 2 * width + i * lanes : 2 * width + (i + 1) * lanes] = ins[3 * i + 2][...]

        @pl.when(t >= middle)
        def _():
            own_ref[...] = y

    rows_in = pl.BlockSpec((tile, lanes), lambda t: ((t + middle) % tiles, 0))
    return pl.pallas_call(
        body,
        out_shape=(
            jax.ShapeDtypeStruct((rows // 2, width), F32),
            jax.ShapeDtypeStruct((rows // 2, 2 * width + half), BF),
        ),
        grid=(tiles,),
        in_specs=[rows_in] * len(flat)
        + [pl.BlockSpec((3, width, half), lambda t: (0, 0, 0))]
        + [pl.BlockSpec((tile, width), lambda t: (jnp.minimum(t, middle - 1), 0))]
        + [anywhere()] * len(deps),
        out_specs=[
            pl.BlockSpec((tile, width), lambda t: (jnp.maximum(t - middle, 0), 0)),
            pl.BlockSpec((tile, 2 * width + half), lambda t: (jnp.minimum(t, middle - 1), 0)),
        ],
        compiler_params=params(VMEM),
        cost_estimate=cost(6 * rows * width * half, 8e6),
    )(*flat, w_all, branch, *deps)


class Grid:
    def __init__(self):
        self.depth = lax.axis_size(NARROW)
        self.wide = lax.axis_size(WIDE)
        self.plane = self.wide // 2
        self.bits = self.plane.bit_length() - 1
        place = lax.axis_index(WIDE)
        self.core = place % 2
        self.chip = place // 2
        self.level = lax.axis_index(NARROW)

    def flip(self, label):
        return sum(((label >> b) & 1) << (self.bits - 1 - b) for b in range(self.bits))

    def chip_of(self, label):
        return self.chip ^ jnp.where(self.core == 0, label, self.flip(label))

    def label_of(self, chip):
        return jnp.where(self.core == 0, self.chip ^ chip, self.flip(self.chip ^ chip))

    def other(self, array):
        return lax.ppermute(array, WIDE, [(i, i ^ 1) for i in range(self.wide)])

    def hop(self, array, bit):
        pairs = []
        for i in range(self.wide):
            step = bit if i % 2 == 0 else self.bits - 1 - bit
            pairs.append((i, i ^ (2 << step)))
        return lax.ppermute(array, WIDE, pairs)

    def lift(self, array, distance):
        return lax.ppermute(array, NARROW, [(i, i ^ distance) for i in range(self.depth)])

    def lifts(self, block, first=None, wait=None):
        out = [block]
        for d in range(1, self.depth):
            low = d & -d
            if d <= 2 and first is not None:
                out.append(first[d - 1])
                continue
            source = out[d ^ low]
            if wait is not None and d != low:
                source = tie(source, wait)
            out.append(self.lift(source, low))
        return out

    def spots(self):
        return jnp.stack(
            [
                (self.level ^ d) * self.plane + self.chip_of(label)
                for label in range(self.plane)
                for d in range(self.depth)
            ]
        ).astype(jnp.int32)

    def spread(self, levels, first=None, wait=None):
        parts = [levels]
        for label in range(1, self.plane):
            top = label.bit_length() - 1
            source = parts[label ^ (1 << top)]
            if first is not None and label in (1, 1 << (self.bits - 1)):
                parts.append(first[0] if label == 1 else first[1])
                continue
            if wait is not None and source is not levels:
                source = tie(source, wait)
            parts.append(self.hop(source, top))
        return parts

    def fold(self, low, high, waits=(), ends=()):
        steps = [self.fold_step(low, high, self.bits - 1, waits[:1], ends[:1])]
        return steps + self.fold_rest(steps[0], waits[1:], ends[1:])

    def fold_rest(self, halves, waits=(), ends=()):
        steps = []
        for bit in range(self.bits - 2, -1, -1):
            n = len(steps)
            halves = self.fold_step(*halves, bit, waits[n : n + 1], ends[n : n + 1])
            steps.append(halves)
        return steps

    def fold_step(self, low, high, bit, waits=(), ends=()):
        for wait in waits:
            high = high if wait is None else tie(high, wait)
        came = self.hop(high, bit)
        for end in ends:
            low = low if end is None else tie(low, end)

        def added(a, b):
            return (a.astype(F32) + b.astype(F32)).astype(BF)

        if low.shape[0] == 1:
            return added(low[0], came[0])
        middle = low.shape[0] // 2
        return added(low[:middle], came[:middle]), added(low[middle:], came[middle:])

    def drop_all(self, blocks, ends=()):
        ends = list(ends)
        steps = []
        bit = 1
        while bit < self.depth:
            pairs = blocks.reshape((-1, 2) + blocks.shape[1:])
            came = self.lift(pairs[:, 1], bit).astype(F32)
            own = pairs[:, 0]
            if ends:
                own = tie(own, *ends.pop(0))
            total = own.astype(F32) + came
            bit *= 2
            blocks = total.astype(BF) if bit < self.depth else total
            steps.append(blocks)
        return steps[:-1] + [blocks[0]]


def tie(array, *deps):
    return lax.optimization_barrier((array,) + deps)[0]


def on_device(
    layer_in,
    first_values,
    out_grad,
    seq_group,
    short_split,
    attn_gain,
    mlp_gain,
    w_query,
    w_key,
    w_value,
    w_out,
    w_gate,
    w_up,
    w_down,
):
    grid = Grid()
    core = grid.core
    rows, width = layer_in.shape
    half = width // 2
    heads = half // HEAD_DIM
    shard = w_query.shape[0]
    block = 2 * shard

    def pick(first, second):
        return jnp.where(core == 0, first, second)

    split_own = jnp.where(seq_group[0] == 0, rows, short_split[0])
    gain_col = attn_gain.astype(F32)[:, None]
    w4 = [(gain_col * w.astype(F32)).astype(BF) for w in (w_query, w_key, w_value)] + [w_out.T]
    spare = jnp.zeros((16, half), BF).at[0, :shard].set(mlp_gain)
    spare = spare.at[1, :2].set(jnp.stack([split_own // 256, split_own % 256]).astype(BF))
    mine = jnp.concatenate([pick(w[:, :half], w[:, half:]) for w in w4] + [spare])
    came = grid.other(
        jnp.concatenate([pick(w[:, half:], w[:, :half]) for w in w4] + [spare])
    )
    split_other = came[4 * shard + 1, :2].astype(jnp.int32)
    split_other = split_other[0] * 256 + split_other[1]
    own_block = assemble(core.reshape(1).astype(jnp.int32), mine, came, shard)

    ff3 = jnp.stack([w_gate.T, w_up.T, w_down])
    units = ff3.shape[1] // 2
    cols = ff3.shape[2]
    ff_mine = pick(ff3[:, :units], ff3[:, units:])
    ff_came = grid.other(pick(ff3[:, units:], ff3[:, :units]))
    ff_block = pick(
        jnp.concatenate([ff_mine, ff_came], 2), jnp.concatenate([ff_came, ff_mine], 2)
    )

    fv_left, fv_right = first_values[:, :half], first_values[:, half:]
    sent = jnp.concatenate([layer_in, pick(fv_right, fv_left)], 1)
    got = grid.other(sent)
    x_other = got[:, :width]
    x2 = jnp.concatenate([layer_in, x_other]).astype(F32)
    fv2 = jnp.concatenate([pick(fv_left, fv_right), got[:, width:]])

    own_block = tie(own_block, got, ff_came)
    near_one = grid.hop(own_block, 0), grid.hop(own_block, grid.bits - 1)
    levels = grid.lifts(own_block)
    ff_own_block = tie(ff_block, *near_one)
    ff_own_one = grid.hop(ff_own_block, 0), grid.hop(ff_own_block, grid.bits - 1)
    level_blocks = tie(jnp.stack(levels[1:]), *near_one, *ff_own_one)
    ff_block_later = tie(ff_block, level_blocks)
    ff_first = grid.lift(ff_block_later, 1)
    far = grid.spread(level_blocks, wait=ff_first)
    near = grid.spread(own_block, first=near_one, wait=far[1])
    ff_own = grid.spread(ff_own_block, first=ff_own_one, wait=far[-1])
    ff_second = grid.lift(ff_block_later, 2)
    chips = jnp.stack([grid.chip_of(m) for m in range(grid.plane)]).astype(jnp.int32)
    spots = grid.spots()

    row_index = jnp.arange(rows, dtype=jnp.int32)
    splits = jnp.stack([split_own, split_other])
    lane = jnp.arange(128) % HEAD_DIM
    frequency = jnp.exp(
        (lane % (HEAD_DIM // 2)).astype(F32) * (-2.0 * math.log(10000.0) / HEAD_DIM)
    )
    second = row_index[None, :] >= splits[:, None]
    position = jnp.where(second, row_index[None, :] - splits[:, None], row_index[None, :])
    turned = position.astype(F32).reshape(-1)[:, None] * frequency[None, :]
    cos = jnp.cos(turned)
    sin = jnp.sin(turned) * jnp.where(lane < HEAD_DIM // 2, -1.0, 1.0)

    inv1 = rms_scale(x2)
    xhat = (x2 * inv1).astype(BF)
    queries, keys, values, w_all, out_mine, gains = project_rows(
        xhat, fv2, cos, sin, near, far, spots, block
    )
    out_other = grid.other(out_mine)
    og_other = grid.other(tie(out_grad, queries))
    ff_one = grid.spread(tie(ff_first, far[-1]), wait=queries)
    ff_third = grid.lift(tie(ff_second, queries), 1)
    ff_second_tied = tie(ff_second, queries)
    ff_two_one = grid.hop(ff_second_tied, 0), grid.hop(ff_second_tied, grid.bits - 1)
    attended, weights = attend(
        splits, queries, keys, values, deps=[ff_own[3], ff_one[1], ff_one[2]]
    )
    ff_two = grid.spread(ff_second_tied, first=ff_two_one, wait=attended)
    att_other = grid.other(attended)

    gain_mlp = gains.reshape(-1, 16, half)[:, :2, :shard].reshape(1, width).astype(F32)
    hidden, normed_two = out_and_norm(
        layer_in, x_other, attended, att_other, out_mine, out_other, gain_mlp
    )

    ff_three = grid.spread(tie(ff_third, normed_two))

    def feed(parts, before=None, deps=()):
        if parts[0][0].shape[-1] % 128 == 0:
            return feed_forward(chips, normed_two, out_grad, og_other, parts, before, deps)
        wholes = []
        for level in parts:
            stacked = jnp.stack(level)
            order = [stacked[grid.label_of(b)] for b in range(grid.plane)]
            wholes.append([jnp.concatenate(order, axis=-1)])
        sums, grads = feed_forward(
            chips, normed_two, out_grad, og_other, wholes, before, deps
        )
        grads = grads[0][0].reshape((3, -1, grid.plane, 2 * cols))
        grads = [grads[..., grid.chip_of(m), :] for m in range(grid.plane)]
        middle = grid.plane // 2
        return sums, [jnp.stack(grads[:middle]), jnp.stack(grads[middle:])]

    sums_a, grads_a = feed([ff_own], deps=[ff_two[2]])
    sums_b, grads_b = feed([ff_one], before=sums_a, deps=[ff_three[1], ff_three[2], ff_two[3]])
    fold_a = grid.fold(*grads_a, waits=[None, sums_b[2]], ends=[sums_b[2]])
    sums, grads_c = feed([ff_two, ff_three], before=sums_b, deps=[fold_a[0][1]])
    branch, branch_sent, grad_nt = sums
    fold_b = [grid.fold_step(*grads_b, grid.bits - 1, ends=[grad_nt])]
    grad_nt_other = grid.other(tie(grad_nt, fold_a[-1], fold_b[0][1]))

    grad_hidden, grad_att, out_low, out_high = norm_two_back(
        spots, grad_nt, grad_nt_other, hidden, out_grad, og_other, gain_mlp,
        attended, out_mine, block, grid.plane,
    )
    pairs = half // 256
    fold_b += grid.fold_rest(fold_b[0], waits=[grad_nt], ends=[grad_att])
    lifted = grid.lift(fold_b[-1], 1)
    back_one = attend_back(
        queries, keys, values, weights, grad_att, cos, sin, 0, pairs, deps=[fold_b[-1]]
    )
    out_fold = [grid.fold_step(out_low, out_high, grid.bits - 1, ends=[back_one[0]])]
    fold_c = grid.fold(*grads_c, waits=[None, back_one[0]], ends=[grad_att])
    first = projection_grads(
        spots, xhat, back_one[:3], block, grid.plane, deps=[fold_c[0][1]]
    )
    back_two = attend_back(
        queries, keys, values, weights, grad_att, cos, sin, 1, pairs,
        deps=[lifted, out_fold[0][1], first[0]],
    )
    second = projection_grads(
        spots, xhat, back_two[:3], block, grid.plane, deps=[fold_c[-1]]
    )
    rest = [fold_c[-1][:, i * units : (i + 1) * units] for i in range(grid.depth - 2)]
    lifted_far = grid.lift(rest[1], 1)
    scaled_own, scaled_sent = rows_grad(
        (back_one[:3], back_two[:3]), w_all, branch_sent, deps=[second[0]]
    )
    second_fold = grid.fold(*second, ends=[scaled_own])
    out_fold += grid.fold_rest(out_fold[0], waits=[back_one[0]], ends=[second[0]])
    first_fold = grid.fold(*first, waits=[None, second[0]], ends=[second[0], second_fold[0][1]])
    got = grid.other(scaled_sent)
    layer_out = hidden[:rows] + branch.astype(F32) + got[:, width : 2 * width].astype(F32)
    layer_out = layer_out.astype(BF)
    scaled_one = scaled_own + got[:, :width].astype(F32)
    v_keep = jnp.concatenate([back_one[3], back_two[3]], 1)
    v_got = got[:, 2 * width :].astype(F32)
    values_grad = pick(
        jnp.concatenate([v_keep, v_got], 1), jnp.concatenate([v_got, v_keep], 1)
    )
    x1 = layer_in.astype(F32)
    i1 = rms_scale(x1)
    in_grad = (
        grad_hidden
        + i1 * scaled_one
        - x1 * (i1 * i1 * i1) * jnp.mean(scaled_one * x1, axis=-1, keepdims=True)
    )
    second_levels = grid.drop_all(
        second_fold[-1], ends=[(scaled_own,), (in_grad, layer_out, values_grad)]
    )
    first_levels = grid.drop_all(first_fold[-1], ends=[(second_fold[-1],), (second_levels[-1],)])
    qkv_total = jnp.concatenate([first_levels[-1], second_levels[-1]], -1)
    qkv_total = qkv_total.reshape(3, block, half)
    out_total = grid.drop_all(out_fold[-1], ends=[(second_fold[0][1],), (second_levels[-1],)])[-1]

    kept = tie(fold_a[-1], second_levels[-1]).astype(F32) + lifted.astype(F32)
    passed = (tie(rest[0], second_fold[0][1]).astype(F32) + lifted_far.astype(F32)).astype(BF)
    total = kept + grid.lift(passed, 2).astype(F32)
    keep = pick(total[:, :, :cols], total[:, :, cols:])
    sent = pick(total[:, :, cols:], total[:, :, :cols]).astype(BF)
    got = grid.other(sent).astype(F32)
    ff_grads = pick(jnp.concatenate([keep, got], 1), jnp.concatenate([got, keep], 1))
    def own_rows(total):
        keep = pick(total[..., :shard, :], total[..., shard:, :])
        got = grid.other(pick(total[..., shard:, :], total[..., :shard, :]).astype(BF))
        got = got.astype(F32)
        return pick(jnp.concatenate([keep, got], -1), jnp.concatenate([got, keep], -1))

    plain = own_rows(qkv_total)
    attn_gain_grad = sum(
        jnp.sum(plain[k] * w.astype(F32), axis=-1)
        for k, w in enumerate((w_query, w_key, w_value))
    )
    out_proj_grad = own_rows(out_total[:block]).T
    gain_total = out_total[block]
    mlp_gain_grad = pick(gain_total[:shard], gain_total[shard : 2 * shard])
    return (
        layer_out,
        in_grad,
        values_grad,
        attn_gain_grad,
        mlp_gain_grad,
        gain_col * plain[0],
        gain_col * plain[1],
        gain_col * plain[2],
        out_proj_grad,
        ff_grads[0].T,
        ff_grads[1].T,
        ff_grads[2],
    )


def solution(mesh):
    rows = P((NARROW, WIDE), None)
    line = P((NARROW, WIDE))
    lanes = P(None, (NARROW, WIDE))
    return jax.shard_map(
        on_device,
        mesh=mesh,
        in_specs=(
            (rows,) * 3 + (line,) * 4 + (rows,) * 3
            + (lanes, P(WIDE, NARROW), P(WIDE, NARROW), P(NARROW, WIDE))
        ),
        out_specs=(
            (rows,) * 3 + (line,) * 2 + (rows,) * 3
            + (lanes, P(WIDE, NARROW), P(WIDE, NARROW), P(NARROW, WIDE))
        ),
        check_vma=False,
    )
```
